256 devices in a mesh: genome: 64 (over y, z_lo, x), maps: 4 (over z_hi, core).
Axes of the slice: x: 4, y: 4, z: 8 (z_hi: 2, z_lo: 4; z = z_hi * 4 + z_lo), core: 2. Of those that a mesh axis runs over, the one named last changes fastest.
Arguments:
- band_maps: bfloat16 [512, 32, 16384], P('maps', None, 'genome'), may hold values from -300 to 300
- stratum_ids: int32 [16], replicated, may hold values from 4 to 27, as said below
- half_width: int32 [16], replicated, may hold values from 1 to 2
Outputs:
- gram: float32 [512, 16, 512], P('genome', None, 'maps')
- scc: float32 [512, 512], P('genome', 'maps')
The draws below stay inside these ranges and needn't reach their ends.
Inputs may be any that keep to these rules, and one draw needn't show every extreme that they name: `stratum_ids`: distinct offsets.
All inputs are finite; a program needn't handle non-finite values.
Results may differ from the reference program's by a relative error of at most 0.0003.
Values may be sent and summed in bfloat16 or wider, within the bound.
No kernel may reach another device: no remote copies, remote signals or barrier semaphores. Data moves between devices by JAX's collectives and lax.ppermute only.
A program may use at most 64 MiB of HBM per device.

```python
import jax
import jax.numpy as jnp
from jax import lax

STRATA = 16
WIDE = 32
HMAX = 2
MAPS = 512
BINS = 16384


def draw_band_maps(key, part):
    key = jax.random.fold_in(key, 5)
    keys = jax.random.split(key, 9)
    key_common, key_own, key_maps, key_rough, key_level, key_pool, key_shape, key_mix, key_order = keys
    offsets = jnp.arange(WIDE, dtype=jnp.float32)
    base = 0.8 * (offsets + 1.0) ** (-0.15)
    position = jnp.arange(BINS, dtype=jnp.float32) / BINS
    trend = 1.0 + 2.0 * position
    common = jax.random.truncated_normal(key_common, -3.0, 3.0, (WIDE, BINS), jnp.float32)
    map_factor = jnp.exp(jax.random.uniform(key_maps, (MAPS, 1, 1), jnp.float32, -0.7, 0.7))
    level = jax.random.uniform(key_level, (MAPS, WIDE, 1), jnp.float32, 0.5, 1.5)
    pool = jax.random.truncated_normal(key_pool, -3.0, 3.0, (MAPS, BINS), jnp.float32)
    profile = jax.random.uniform(key_shape, (MAPS, WIDE), jnp.float32, 0.5, 1.5)
    order = jax.random.permutation(key_order, MAPS).astype(jnp.int32)
    own = jax.random.truncated_normal(key_own, -4.0, 4.0, (MAPS, WIDE, BINS), jnp.float32)
    rough = jnp.exp(jax.random.uniform(key_rough, (BINS,), jnp.float32, -0.7, 0.7))
    mixing = jax.random.truncated_normal(key_mix, -2.5, 2.5, (MAPS, 8), jnp.float32)
    latent = jnp.zeros((MAPS, WIDE, BINS), jnp.float32)
    for turn in range(8):
        picked = (order + turn) % MAPS
        latent = latent + mixing[:, turn, None, None] * profile[picked][:, :, None] * pool[picked][:, None, :]
    scale = base[:, None] * (trend * rough)[None, :]
    inner = level + 0.4 * common[None, :, :] + latent * 8.0 ** (-0.5) + 0.9 * own
    values = scale[None, :, :] * map_factor * inner
    return jnp.clip(values, -300.0, 300.0).astype(jnp.bfloat16)


def draw_stratum_ids(key, part):
    key = jax.random.fold_in(key, 11)
    key_pick, key_order = jax.random.split(key, 2)
    middle = jax.random.permutation(key_pick, WIDE - 4 * HMAX - 2)[:STRATA - 2] + 2 * HMAX + 1
    ends = jnp.array([2 * HMAX, WIDE - 2 * HMAX - 1], jnp.int32)
    picked = jnp.concatenate([ends, middle.astype(jnp.int32)])
    return jax.random.permutation(key_order, picked).astype(jnp.int32)


def place_ends(values, own_key, least, top_value):
    longest = values.shape.index(max(values.shape))
    spots = []
    for shift in (0, 1):
        where = [jax.random.randint(jax.random.fold_in(own_key, axis), (), 0, length) for axis, length in enumerate(values.shape)]
        where[longest] = (where[longest] + shift) % values.shape[longest]
        spots.append(tuple(where))
    return values.at[spots[0]].set(least).at[spots[1]].set(top_value)


def setup_inputs(seed: int = 0) -> dict:
    streams_of = jax.random.split(jax.random.key(seed), 4)
    band_maps = draw_band_maps(jax.random.fold_in(streams_of[3], 71), 0)
    stratum_ids = draw_stratum_ids(jax.random.fold_in(streams_of[3], 71), 0)
    half_width = place_ends(jax.random.randint(streams_of[2], (STRATA,), 1, HMAX + 1), jax.random.fold_in(streams_of[2], 1), 1, HMAX).astype(jnp.int32)
    return dict(band_maps=band_maps, stratum_ids=stratum_ids, half_width=half_width)


def reference(band_maps, stratum_ids, half_width):
    num_maps = band_maps.shape[0]
    num_bins = band_maps.shape[2]
    padded = jnp.pad(band_maps, ((0, 0), (0, 0), (HMAX, HMAX)))

    def per_stratum(pair):
        stratum, radius = pair
        weights = [(jnp.abs(jnp.int32(lag)) <= radius).astype(jnp.float32) for lag in range(-HMAX, HMAX + 1)]
        window = (2 * radius + 1).astype(jnp.float32)
        norm_area = window * window
        slab = lax.dynamic_slice_in_dim(padded, (stratum - 2 * HMAX).astype(jnp.int32), 4 * HMAX + 1, 1).astype(jnp.float32)
        smooth = jnp.zeros((num_maps, num_bins), jnp.float32)
        for across in range(-HMAX, HMAX + 1):
            for along in range(-HMAX, HMAX + 1):
                factor = weights[across + HMAX] * weights[along + HMAX]
                smooth = smooth + factor * slab[:, 2 * HMAX + along - across, HMAX + across:HMAX + across + num_bins]
        smooth = smooth / norm_area
        centre = lax.optimization_barrier(jnp.sum(smooth, axis=1)) / num_bins
        deviation = smooth - centre[:, None]
        spread = lax.optimization_barrier(jnp.sum(deviation * deviation, axis=1)) / num_bins
        centered = deviation.astype(jnp.bfloat16)
        gram_one = jnp.dot(centered, centered.T, preferred_element_type=jnp.float32) / num_bins
        return (gram_one, spread)
    grams, spreads = lax.map(per_stratum, (stratum_ids, half_width))
    gram_out = jnp.transpose(grams, (1, 0, 2))
    denominator = lax.optimization_barrier(jnp.sum(jnp.sqrt(spreads[:, :, None] * spreads[:, None, :]), axis=0))
    scc = lax.optimization_barrier(jnp.sum(gram_out, axis=1)) / denominator
    return (gram_out, scc)
```

```python
import jax
import jax.numpy as jnp
from jax import lax
from jax.experimental import pallas as pl
from jax.experimental.pallas import tpu as pltpu
from jax.sharding import Mesh, PartitionSpec as P

HMAX = 2
BINS_AXES = ("y", "zl", "x")
MAPS_AXES = ("zh", "core")
STRATA_AXES = ("zl", "zh", "core")
SUM_AXES = ("y", "x")
F32 = jnp.float32
BF16 = jnp.bfloat16
HEAD = 8
VMEM_LIMIT = 32 * 1024 * 1024


def params():
    return pltpu.CompilerParams(vmem_limit_bytes=VMEM_LIMIT)


def edge_kernel(band_ref, edge_ref):
    maps, wide, bins = band_ref.shape
    rows = maps * wide
    data = band_ref[...].reshape(rows, bins)
    column = lax.broadcasted_iota(jnp.int32, (bins, 128), 0)
    part = lax.rem(lax.broadcasted_iota(jnp.int32, (bins, 128), 1), 4)
    pick = (column == jnp.where(part < 2, bins - 2 + part, part - 2)).astype(BF16)
    spread = jnp.dot(data, pick, preferred_element_type=F32).reshape(maps, wide, 128)
    offset = lax.broadcasted_iota(jnp.int32, (wide, 128), 0)
    lane = lax.broadcasted_iota(jnp.int32, (wide, 128), 1)
    spread = jnp.where((lax.div(lane, 4) == offset)[None], spread, 0.0)
    spread = spread.astype(BF16).reshape(rows, 128)
    m = lax.broadcasted_iota(jnp.int32, (maps, rows), 0)
    r = lax.broadcasted_iota(jnp.int32, (maps, rows), 1)
    gather = (lax.div(r, wide) == m).astype(BF16)
    edge_ref[...] = jnp.dot(gather, spread, preferred_element_type=F32).astype(BF16)


def edges(band_maps):
    maps, wide, bins = band_maps.shape
    step = 32
    return pl.pallas_call(
        edge_kernel,
        grid=(maps // step,),
        in_specs=[pl.BlockSpec((step, wide, bins), lambda i: (i, 0, 0))],
        out_specs=pl.BlockSpec((step, 128), lambda i: (i, 0)),
        out_shape=jax.ShapeDtypeStruct((maps, 128), BF16),
        compiler_params=params(),
        name="edges",
    )(band_maps)


def smooth_kernel(ids_ref, half_ref, band_ref, low_ref, high_ref, out_ref, plane_ref, turned_ref, win_ref, perm_ref):
    maps, wide, bins = band_ref.shape
    strata = out_ref.shape[0]
    r = lax.broadcasted_iota(jnp.int32, (8 * wide, 8 * wide), 0)
    c = lax.broadcasted_iota(jnp.int32, (8 * wide, 8 * wide), 1)
    perm_ref[...] = (c == lax.rem(r, 8) * wide + lax.div(r, 8)).astype(BF16)
    for g in range(maps // 8):
        group = jnp.dot(
            perm_ref[...], band_ref[pl.ds(8 * g, 8)].reshape(8 * wide, bins), preferred_element_type=F32
        )
        plane_ref[:, pl.ds(8 * g, 8), :] = group.reshape(wide, 8, bins)

    low = jnp.transpose(low_ref[...].astype(F32))
    high = jnp.transpose(high_ref[...].astype(F32))
    for d in range(wide):
        turned_ref[d, pl.ds(HEAD - 2, 2), :] = low[4 * d : 4 * d + 2, :]
        turned_ref[d, pl.ds(HEAD + bins, 2), :] = high[4 * d + 2 : 4 * d + 4, :]

    def turn(d, carry):
        for half in range(bins // 128):
            tile = plane_ref[d, :, half * 128 : half * 128 + 128]
            turned_ref[d, pl.ds(HEAD + half * 128, 128), :] = jnp.transpose(tile)
        return carry

    lax.fori_loop(0, wide, turn, 0, unroll=4)

    def windows(i, carry):
        rows = pl.ds(pl.multiple_of(i * 16, 16), 16)
        planes = [turned_ref[d, rows, :] for d in range(wide)]
        for mid in range(1, wide - 1):
            one = planes[mid - 1] + planes[mid] + planes[mid + 1]
            win_ref[0, mid, rows, :] = one
            if 2 <= mid < wide - 2:
                win_ref[1, mid, rows, :] = one + (planes[mid - 2] + planes[mid + 2])
        return carry

    lax.fori_loop(0, turned_ref.shape[1] // 16, windows, 0)

    row = lax.broadcasted_iota(jnp.int32, (16, maps), 0)
    step = 64

    def stratum(k, carry):
        wider = half_ref[k] >= 2
        h = jnp.where(wider, 1, 0)
        reach = jnp.where(wider, 2, 0)
        outer = jnp.where(wider, 1.0, 0.0)
        scale = jnp.where(wider, 1.0 / 25.0, 1.0 / 9.0)
        centre = ids_ref[k]
        parts = []
        total = jnp.zeros((1, maps), F32)
        for i in range(bins // step):
            at = HEAD + i * step
            acc = win_ref[h, centre, pl.ds(at, step), :]
            acc = acc + win_ref[h, centre + 1, pl.ds(at - 1, step), :]
            acc = acc + win_ref[h, centre - 1, pl.ds(at + 1, step), :]
            far = win_ref[h, centre + reach, pl.ds(at - 2, step), :] + win_ref[h, centre - reach, pl.ds(at + 2, step), :]
            acc = (acc + far * outer) * scale
            parts.append(acc)
            total = total + jnp.sum(acc, axis=0, keepdims=True)
        mean = total * (1.0 / bins)
        for i, acc in enumerate(parts):
            out_ref[k, pl.ds(i * step, step), :] = (acc - mean).astype(BF16)
        hi = mean.astype(BF16).astype(F32)
        mid = (mean - hi).astype(BF16).astype(F32)
        low = mean - hi - mid
        side = jnp.where(row == 0, hi, jnp.where(row == 1, mid, jnp.where(row == 2, low, 0.0)))
        out_ref[k, pl.ds(bins, 16), :] = side.astype(BF16)
        return carry

    lax.fori_loop(0, strata, stratum, 0, unroll=2)


def smoothed(band_maps, low, high, stratum_ids, half_width):
    maps, wide, bins = band_maps.shape
    strata = stratum_ids.shape[0]
    rows = bins + 16
    smem = pl.BlockSpec(memory_space=pltpu.SMEM)
    vmem = pl.BlockSpec(memory_space=pltpu.VMEM)
    return pl.pallas_call(
        smooth_kernel,
        in_specs=[smem, smem, vmem, vmem, vmem],
        out_specs=vmem,
        out_shape=jax.ShapeDtypeStruct((strata, rows, 128), BF16),
        scratch_shapes=[
            pltpu.VMEM((wide, maps, bins), F32),
            pltpu.VMEM((wide, bins + 2 * HEAD, maps), F32),
            pltpu.VMEM((2, wide, bins + 2 * HEAD, maps), F32),
            pltpu.VMEM((8 * wide, 8 * wide), BF16),
        ],
        compiler_params=params(),
        name="smooth",
    )(stratum_ids, half_width, band_maps, low, high)


def dot_tn(a, b):
    return lax.dot_general(
        a, b, (((0,), (0,)), ((), ())), precision=lax.Precision.HIGHEST, preferred_element_type=F32
    )


def gram_kernel(blocks, panels, sum_y, sum_x, bins, in_ref, out_ref, data_ref, mean_ref, gram_ref):
    maps = 128
    total = panels * maps
    mean_ref[...] = jnp.zeros_like(mean_ref)
    for z in range(blocks):
        for m in range(panels):
            src = z * panels + m
            data_ref[pl.ds(z * bins, bins), pl.ds(m * maps, maps)] = in_ref[src, pl.ds(0, bins), :]
            words = in_ref[src, pl.ds(bins, 16), :].astype(F32)
            mean_ref[z : z + 1, m * maps : (m + 1) * maps] = words[0:1] + words[1:2] + words[2:3]
    means = mean_ref[...]
    centre = jnp.sum(means, axis=0, keepdims=True) * (1.0 / blocks)
    row = lax.broadcasted_iota(jnp.int32, means.shape, 0)
    dev = jnp.where(row < blocks, means - centre, 0.0)
    data = data_ref[...]
    gram_ref[...] = lax.dot_general(
        data, data, (((0,), (0,)), ((), ())), preferred_element_type=F32
    ) + dot_tn(dev, dev) * float(bins)
    r = lax.broadcasted_iota(jnp.int32, (maps, maps), 0)
    c = lax.broadcasted_iota(jnp.int32, (maps, maps), 1)
    side = [centre[:, m * maps : (m + 1) * maps] for m in range(panels)]
    for m in range(panels):
        block = gram_ref[pl.ds(m * maps, maps), pl.ds(m * maps, maps)]
        side.append(jnp.sum(jnp.where(r == c, block, 0.0), axis=0, keepdims=True))
    side = jnp.concatenate(side, axis=0)
    per = maps // (blocks * sum_x)
    for y in range(sum_y):
        for x in range(sum_x):
            d = y * sum_x + x
            for m in range(panels):
                for z in range(blocks):
                    q = y * maps + (z * sum_x + x) * per
                    out_ref[d, pl.ds((m * blocks + z) * per, per), :] = gram_ref[
                        pl.ds(q, per), pl.ds(m * maps, maps)
                    ]
            out_ref[d, pl.ds(panels * blocks * per, 2 * panels), :] = side


def partial_gram(received, blocks, panels, sum_y, sum_x):
    bins = received.shape[1] - 16
    total = panels * 128
    per = 128 // (blocks * sum_x)
    vmem = pl.BlockSpec(memory_space=pltpu.VMEM)
    return pl.pallas_call(
        lambda *refs: gram_kernel(blocks, panels, sum_y, sum_x, bins, *refs),
        in_specs=[vmem],
        out_specs=vmem,
        out_shape=jax.ShapeDtypeStruct(
            (sum_y * sum_x, panels * blocks * per + 2 * panels, 128), F32
        ),
        scratch_shapes=[
            pltpu.VMEM((blocks * bins, total), BF16),
            pltpu.VMEM((8, total), F32),
            pltpu.VMEM((total, total), F32),
        ],
        compiler_params=params(),
        name="partial_gram",
    )(received)


def sum_kernel(blocks, panels, sum_x, count, in_ref, out_ref, mean_ref, between_ref, spread_ref):
    maps = 128
    parts = in_ref.shape[0]
    rows = in_ref.shape[1] - 2 * panels
    per = rows // (panels * blocks)
    total_bins = float(count * parts)
    for m in range(panels):
        mean_ref[:, m * maps : (m + 1) * maps] = jnp.concatenate(
            [in_ref[d, pl.ds(rows + m, 1), :] for d in range(parts)], axis=0
        )
    means = mean_ref[...]
    dev = means - jnp.sum(means, axis=0, keepdims=True) * (1.0 / parts)
    own = jnp.concatenate(
        [
            sum(in_ref[d, pl.ds(rows + panels + m, 1), :] for d in range(parts))
            for m in range(panels)
        ],
        axis=1,
    )
    spread = (own + float(count) * jnp.sum(dev * dev, axis=0, keepdims=True)) * (1.0 / total_bins)
    y = lax.axis_index("y")
    x = lax.axis_index("x")
    for m in range(panels):

        @pl.when(y == m)
        def _():
            cols = slice(m * maps, (m + 1) * maps)
            between_ref[...] = dot_tn(dev[:, cols], dev) * float(count)
            spread_ref[...] = jnp.transpose(jnp.broadcast_to(spread[:, cols], (maps, maps)))

    for z in range(blocks):
        start = pl.multiple_of((z * sum_x + x) * per, per)
        between = between_ref[pl.ds(start, per), :]
        spread_q = spread_ref[pl.ds(start, per), :]
        for m in range(panels):
            tile = pl.ds((m * blocks + z) * per, per)
            acc = in_ref[0, tile, :]
            for d in range(1, parts):
                acc = acc + in_ref[d, tile, :]
            cols = slice(m * maps, (m + 1) * maps)
            out_ref[z * panels + m, pl.ds(0, per), :] = (acc + between[:, cols]) * (1.0 / total_bins)
            out_ref[z * panels + m, pl.ds(per, per), :] = jnp.sqrt(spread_q * spread[:, cols])


def summed(received, blocks, panels, sum_x, count):
    parts = received.shape[0]
    per = (received.shape[1] - 2 * panels) // (panels * blocks)
    vmem = pl.BlockSpec(memory_space=pltpu.VMEM)
    return pl.pallas_call(
        lambda *refs: sum_kernel(blocks, panels, sum_x, count, *refs),
        in_specs=[vmem],
        out_specs=vmem,
        out_shape=jax.ShapeDtypeStruct((blocks * panels, 2 * per, 128), F32),
        scratch_shapes=[
            pltpu.VMEM((parts, panels * 128), F32),
            pltpu.VMEM((128, panels * 128), F32),
            pltpu.VMEM((128, 128), F32),
        ],
        compiler_params=params(),
        name="sum_parts",
    )(received)


def final_kernel(in_ref, gram_ref, scc_ref):
    strata, rows, _ = in_ref.shape
    per = rows // 2
    top = jnp.zeros((per, 128), F32)
    bottom = jnp.zeros((per, 128), F32)
    for k in range(strata):
        tile = in_ref[k, pl.ds(0, per), :]
        gram_ref[:, k, :] = tile
        top = top + tile
        bottom = bottom + in_ref[k, pl.ds(per, per), :]
    scc_ref[...] = top / bottom


def final(received):
    strata, rows, lanes = received.shape
    vmem = pl.BlockSpec(memory_space=pltpu.VMEM)
    return pl.pallas_call(
        final_kernel,
        in_specs=[vmem],
        out_specs=[vmem, vmem],
        out_shape=[
            jax.ShapeDtypeStruct((rows // 2, strata, lanes), F32),
            jax.ShapeDtypeStruct((rows // 2, lanes), F32),
        ],
        compiler_params=params(),
        name="final",
    )(received)


def body(band_maps, stratum_ids, half_width):
    maps, wide, bins = band_maps.shape
    blocks, sum_y, sum_x = (lax.axis_size(a) for a in ("zl", "y", "x"))
    panels = lax.axis_size(MAPS_AXES)
    genome = lax.axis_size(BINS_AXES)
    edge = edges(band_maps)
    forward = [(i, i + 1) for i in range(genome - 1)]
    backward = [(i + 1, i) for i in range(genome - 1)]
    low = lax.ppermute(edge, BINS_AXES, forward)
    high = lax.ppermute(edge, BINS_AXES, backward)
    strata = smoothed(band_maps, low, high, stratum_ids, half_width)
    strata = lax.all_to_all(strata, STRATA_AXES, 0, 0, tiled=True)
    parts = partial_gram(strata, blocks, panels, sum_y, sum_x)
    parts = lax.all_to_all(parts, SUM_AXES, 0, 0, tiled=True)
    tiles = summed(parts, blocks, panels, sum_x, blocks * bins)
    tiles = lax.all_to_all(tiles, STRATA_AXES, 0, 0, tiled=True)
    gram, scc = final(tiles)
    return gram, scc


def solution(mesh):
    split = Mesh(mesh.devices.reshape(4, 4, 4, 2, 2), BINS_AXES + MAPS_AXES)
    in_specs = (P(MAPS_AXES, None, BINS_AXES), P(), P())
    out_specs = (P(BINS_AXES, None, MAPS_AXES), P(BINS_AXES, MAPS_AXES))
    return jax.shard_map(body, mesh=split, in_specs=in_specs, out_specs=out_specs, check_vma=False)
```

```python
import jax
import jax.numpy as jnp
from jax import lax
from jax.experimental import pallas as pl
from jax.experimental.pallas import tpu as pltpu
from jax.sharding import Mesh, PartitionSpec as P

HMAX = 2
BINS_AXES = ("y", "zl", "x")
MAPS_AXES = ("zh", "core")
HALO_AXES = ("y", "zl", "x", "zh")
STRATA_AXES = ("zh", "zl", "core")
SUM_AXES = ("x", "y")
F32 = jnp.float32
BF16 = jnp.bfloat16
HALO = 4
TAIL = 8
RIM = 2
SIDE = 2 + 2 * RIM
VMEM_LIMIT = 28 * 1024 * 1024


def place(z, m, blocks, cores):
    return ((m // cores) * blocks + z) * cores + m % cores


def next_to_here():
    _, zl, x, zh = (lax.axis_size(a) for a in HALO_AXES)
    pairs = []
    for y in range(lax.axis_size("y")):
        flat = [((y * zl + p // x % zl) * x + p % x) * zh + p // (x * zl) for p in range(zh * zl * x)]
        pairs += [(flat[(p + 1) % len(flat)], flat[p]) for p in range(len(flat))]
    return pairs


def params():
    return pltpu.CompilerParams(vmem_limit_bytes=VMEM_LIMIT)


def edge_kernel(band_ref, edge_ref, copy_ref, sems):
    maps, wide, bins = band_ref.shape
    parts = sems.shape[1]
    each = maps // parts
    copies = [
        [
            pltpu.make_async_copy(
                band_ref.at[pl.ds(i * each, each), :, pl.ds(first, size)],
                copy_ref.at[pl.ds(i * each, each), :, pl.ds(first, size)],
                sems.at[half, i],
            )
            for i in range(parts)
        ]
        for half, (first, size) in enumerate(((0, 128), (128, bins - 128)))
    ]
    for copy in copies[0] + copies[1]:
        copy.start()
    column = lax.broadcasted_iota(jnp.int32, (128, 128), 0)
    part = lax.rem(lax.broadcasted_iota(jnp.int32, (128, 128), 1), HALO)
    pick = (column == part).astype(BF16)
    offset = lax.broadcasted_iota(jnp.int32, (wide, 128), 0)
    lane = lax.broadcasted_iota(jnp.int32, (wide, 128), 1)
    own = (lax.div(lane, HALO) == offset)[None]
    rows = each * wide
    m = lax.broadcasted_iota(jnp.int32, (each, rows), 0)
    r = lax.broadcasted_iota(jnp.int32, (each, rows), 1)
    gather = (lax.div(r, wide) == m).astype(BF16)
    for i, copy in enumerate(copies[0]):
        copy.wait()
        data = copy_ref[pl.ds(i * each, each), :, pl.ds(0, 128)].reshape(rows, 128)
        spread = jnp.dot(data, pick, preferred_element_type=F32).reshape(each, wide, 128)
        spread = jnp.where(own, spread, 0.0).astype(BF16).reshape(rows, 128)
        edge = jnp.dot(gather, spread, preferred_element_type=F32)
        edge_ref[pl.ds(i * each, each), :] = edge.astype(BF16)
    for copy in copies[1]:
        copy.wait()


def edges(band_maps):
    maps, wide, bins = band_maps.shape
    vmem = pl.BlockSpec(memory_space=pltpu.VMEM)
    return pl.pallas_call(
        edge_kernel,
        in_specs=[pl.BlockSpec(memory_space=pltpu.HBM)],
        out_specs=[vmem, vmem],
        out_shape=[
            jax.ShapeDtypeStruct((maps, 128), BF16),
            jax.ShapeDtypeStruct(band_maps.shape, BF16),
        ],
        scratch_shapes=[pltpu.SemaphoreType.DMA((2, 4))],
        compiler_params=params(),
        cost_estimate=pl.CostEstimate(flops=2 * maps * wide * 128 * 160, bytes_accessed=2**22, transcendentals=0),
        name="edges",
    )(band_maps)


def windows(planes, win_ref, rows):
    wide = len(planes)
    for mid in range(1, wide - 1):
        one = planes[mid - 1] + planes[mid] + planes[mid + 1]
        win_ref[0, mid, rows, :] = one
        if 2 <= mid < wide - 2:
            win_ref[1, mid, rows, :] = one + (planes[mid - 2] + planes[mid + 2])


def box_of(win_ref, wider, centre):
    h = jnp.where(wider, 1, 0)
    reach = jnp.where(wider, 2, 0)
    outer = jnp.where(wider, 1.0, 0.0)
    scale = jnp.where(wider, 1.0 / 25.0, 1.0 / 9.0)

    def box(at, size):
        acc = win_ref[h, centre, pl.ds(at, size), :]
        acc = acc + win_ref[h, centre + 1, pl.ds(at - 1, size), :]
        acc = acc + win_ref[h, centre - 1, pl.ds(at + 1, size), :]
        far = win_ref[h, centre + reach, pl.ds(at - 2, size), :]
        far = far + win_ref[h, centre - reach, pl.ds(at + 2, size), :]
        return (acc + far * outer) * scale

    return box


def inner_kernel(
    ids_ref, half_ref, band_ref, sums_ref, total_ref, first_win_ref, last_win_ref, plane_ref, turned_ref, win_ref, perm_ref
):
    maps, wide, bins = band_ref.shape
    strata = sums_ref.shape[0]
    r = lax.broadcasted_iota(jnp.int32, (8 * wide, 8 * wide), 0)
    c = lax.broadcasted_iota(jnp.int32, (8 * wide, 8 * wide), 1)
    perm_ref[...] = (c == lax.rem(r, 8) * wide + lax.div(r, 8)).astype(BF16)
    for g in range(maps // 8):
        group = jnp.dot(
            perm_ref[...], band_ref[pl.ds(8 * g, 8)].reshape(8 * wide, bins), preferred_element_type=F32
        )
        plane_ref[:, pl.ds(8 * g, 8), :] = group.reshape(wide, 8, bins)

    def turn(d, carry):
        for half in range(bins // 128):
            tile = plane_ref[d, :, half * 128 : half * 128 + 128]
            turned_ref[d, pl.ds(half * 128, 128), :] = jnp.transpose(tile)
        return carry

    lax.fori_loop(0, wide, turn, 0, unroll=4)

    def some(i, carry):
        rows = pl.ds(pl.multiple_of(i * 16, 16), 16)
        windows([turned_ref[d, rows, :] for d in range(wide)], win_ref, rows)
        return carry

    lax.fori_loop(0, bins // 16, some, 0)
    first_win_ref[...] = win_ref[:, :, pl.ds(0, 8), :]
    last_win_ref[...] = win_ref[:, :, pl.ds(bins - 8, 8), :]

    def stratum(k, carry):
        box = box_of(win_ref, half_ref[k] >= 2, ids_ref[k])
        total = jnp.zeros((1, maps), F32)
        for at in range(0, bins - TAIL, 64):
            size = min(64, bins - TAIL - at)
            part = box(at + 2, size)
            sums_ref[k, pl.ds(at, size), :] = part
            total = total + jnp.sum(part, axis=0, keepdims=True)
        total_ref[k] = jnp.broadcast_to(total, (8, maps))
        return carry

    lax.fori_loop(0, strata, stratum, 0, unroll=2)


def inner(band_maps, stratum_ids, half_width):
    maps, wide, bins = band_maps.shape
    strata = stratum_ids.shape[0]
    smem = pl.BlockSpec(memory_space=pltpu.SMEM)
    vmem = pl.BlockSpec(memory_space=pltpu.VMEM)
    return pl.pallas_call(
        inner_kernel,
        in_specs=[smem, smem, vmem],
        out_specs=[vmem, vmem, vmem, vmem],
        out_shape=[
            jax.ShapeDtypeStruct((strata, bins - TAIL, maps), F32),
            jax.ShapeDtypeStruct((strata, 8, maps), F32),
            jax.ShapeDtypeStruct((2, wide, 8, maps), F32),
            jax.ShapeDtypeStruct((2, wide, 8, maps), F32),
        ],
        scratch_shapes=[
            pltpu.VMEM((wide, maps, bins), F32),
            pltpu.VMEM((wide, bins, maps), F32),
            pltpu.VMEM((2, wide, bins, maps), F32),
            pltpu.VMEM((8 * wide, 8 * wide), BF16),
        ],
        compiler_params=params(),
        cost_estimate=pl.CostEstimate(flops=2 * maps * wide * bins * 256, bytes_accessed=2**22, transcendentals=0),
        name="inner",
    )(stratum_ids, half_width, band_maps)


def words_of(value):
    hi = value.astype(BF16).astype(F32)
    mid = (value - hi).astype(BF16).astype(F32)
    return hi, mid, value - hi - mid


def smooth_kernel(
    ids_ref, half_ref, sums_ref, total_ref, first_win_ref, last_win_ref, next_ref, out_ref, win_ref, start_ref
):
    strata, ready, maps = sums_ref.shape
    wide = first_win_ref.shape[1]
    bins = ready + TAIL
    y, z, x = (lax.axis_index(a) for a in BINS_AXES)
    last_y, last_z, last_x = (lax.axis_size(a) - 1 for a in BINS_AXES)
    before = (z == last_z) & (x == last_x)
    after = (z == 0) & (x == 0)
    ahead = jnp.where(before, 0.0, jnp.transpose(next_ref[...].astype(F32)))
    row8 = lax.broadcasted_iota(jnp.int32, (8, maps), 0)
    tails = []
    for d in range(wide):
        at = HALO * d
        tile = pltpu.roll(ahead[at // 8 * 8 : at // 8 * 8 + 8], (-(at % 8)) % 8, axis=0)
        tails.append(jnp.where(row8 < HALO, tile, 0.0))
    win_ref[:, :, pl.ds(0, 8), :] = last_win_ref[...]
    windows(tails, win_ref, pl.ds(8, 8))
    start_ref[:, :, pl.ds(0, 8), :] = jnp.zeros((2, wide, 8, maps), F32)
    start_ref[:, :, pl.ds(8, 8), :] = first_win_ref[...]

    row = lax.broadcasted_iota(jnp.int32, (16, maps), 0)
    empty = before & (row8 >= 8 - 2 * RIM)
    seam_before = before & (row8 < 2 * RIM) & ((y < last_y) | (row8 < RIM))
    seam_after = after & (row8 < 2 * RIM) & ((y > 0) | (row8 >= RIM))
    per_slot = jnp.where(before, 1.0 / (bins - 2 * RIM), 1.0 / bins)

    def stratum(k, carry):
        wider, centre = half_ref[k] >= 2, ids_ref[k]
        end = box_of(win_ref, wider, centre)(2, 8)
        total = total_ref[k][:1] + jnp.sum(jnp.where(empty, 0.0, end), axis=0, keepdims=True)
        mean = total * per_slot
        for at in range(0, bins, 64):
            size = min(64, ready - at)
            part = sums_ref[k, pl.ds(at, size), :]
            if size < 64:
                part = jnp.concatenate([part, jnp.where(empty, mean, end)], axis=0)
            out_ref[k, pl.ds(at, 64), :] = (part - mean).astype(BF16)
        seam = jnp.where(seam_before, pltpu.roll(end, 2 * RIM, axis=0), 0.0)
        seam = seam + jnp.where(seam_after, box_of(start_ref, wider, centre)(8 - RIM, 8), 0.0)
        side = jnp.zeros((16, maps), F32)
        for i, (m, v) in enumerate(zip(words_of(mean), words_of(seam))):
            v = jnp.concatenate([v, jnp.zeros((8, maps), F32)], axis=0)
            side = jnp.where(row == i, m, side) + pltpu.roll(v, 3 + 2 * RIM * i, axis=0)
        out_ref[k, pl.ds(bins, 16), :] = side.astype(BF16)
        return carry

    lax.fori_loop(0, strata, stratum, 0, unroll=2)


def smoothed(sums, total, first_win, last_win, ahead, stratum_ids, half_width):
    strata, ready, maps = sums.shape
    wide = first_win.shape[1]
    smem = pl.BlockSpec(memory_space=pltpu.SMEM)
    vmem = pl.BlockSpec(memory_space=pltpu.VMEM)
    return pl.pallas_call(
        smooth_kernel,
        in_specs=[smem, smem] + [vmem] * 5,
        out_specs=vmem,
        out_shape=jax.ShapeDtypeStruct((strata, ready + TAIL + 16, maps), BF16),
        scratch_shapes=[
            pltpu.VMEM((2, wide, 16, maps), F32),
            pltpu.VMEM((2, wide, 16, maps), F32),
        ],
        compiler_params=params(),
        name="smooth",
    )(stratum_ids, half_width, sums, total, first_win, last_win, ahead)


def dot_tn(a, b):
    return lax.dot_general(
        a, b, (((0,), (0,)), ((), ())), precision=lax.Precision.HIGHEST, preferred_element_type=F32
    )


def gram_kernel(blocks, panels, cores, sum_y, sum_x, bins, in_ref, out_ref, data_ref, mean_ref, gram_ref):
    maps = 128
    total = panels * maps
    seam = []
    for m in range(panels):
        parts = []
        for z in range(blocks):
            src = place(z, m, blocks, cores)
            data_ref[pl.ds(z * bins, bins), pl.ds(m * maps, maps)] = in_ref[src, pl.ds(0, bins), :]
            words = in_ref[src, pl.ds(bins, 16), :].astype(F32)
            mean_ref[z : z + 1, m * maps : (m + 1) * maps] = words[0:1] + words[1:2] + words[2:3]
            parts.append(words[3:7] + words[7:11] + words[11:15])
        seam.append(sum(parts))
    means = mean_ref[:blocks, :]
    short = lax.axis_index("x") == sum_x - 1
    z = lax.broadcasted_iota(jnp.int32, (blocks, 1), 0)
    count = jnp.where(short & (z == blocks - 1), float(bins - 2 * RIM), float(bins))
    centre = jnp.sum(means * count, axis=0, keepdims=True)
    centre = centre * jnp.where(short, 1.0 / (blocks * bins - 2 * RIM), 1.0 / (blocks * bins))
    dev = means - centre
    hi, mid, low = words_of(dev)
    left_hi, left_mid, left_low = words_of(dev * count)
    empty = jnp.zeros((32 - 6 * blocks, total), F32)
    left = jnp.concatenate([left_hi, left_hi, left_mid, left_mid, left_hi, left_low, empty], axis=0)
    right = jnp.concatenate([hi, mid, hi, mid, low, hi, empty], axis=0)
    tn = (((0,), (0,)), ((), ()))
    data = data_ref[...]
    gram_ref[...] = lax.dot_general(data, data, tn, preferred_element_type=F32) + lax.dot_general(
        left.astype(BF16), right.astype(BF16), tn, preferred_element_type=F32
    )
    r = lax.broadcasted_iota(jnp.int32, (maps, maps), 0)
    c = lax.broadcasted_iota(jnp.int32, (maps, maps), 1)
    side = [centre[:, m * maps : (m + 1) * maps] for m in range(panels)]
    for m in range(panels):
        block = gram_ref[pl.ds(m * maps, maps), pl.ds(m * maps, maps)]
        side.append(jnp.sum(jnp.where(r == c, block, 0.0), axis=0, keepdims=True))
    side = jnp.concatenate(side + seam, axis=0)
    per = maps // (blocks * sum_x)
    for y in range(sum_y):
        for x in range(sum_x):
            d = x * sum_y + y
            for m in range(panels):
                for z in range(blocks):
                    q = y * maps + (z * sum_x + x) * per
                    out_ref[d, pl.ds((m * blocks + z) * per, per), :] = gram_ref[
                        pl.ds(q, per), pl.ds(m * maps, maps)
                    ]
            out_ref[d, pl.ds(panels * blocks * per, SIDE * panels), :] = side


def partial_gram(received, blocks, panels, cores, sum_y, sum_x):
    bins = received.shape[1] - 16
    total = panels * 128
    per = 128 // (blocks * sum_x)
    vmem = pl.BlockSpec(memory_space=pltpu.VMEM)
    return pl.pallas_call(
        lambda *refs: gram_kernel(blocks, panels, cores, sum_y, sum_x, bins, *refs),
        in_specs=[vmem],
        out_specs=vmem,
        out_shape=jax.ShapeDtypeStruct(
            (sum_y * sum_x, panels * blocks * per + SIDE * panels, 128), F32
        ),
        scratch_shapes=[
            pltpu.VMEM((blocks * bins, total), BF16),
            pltpu.VMEM((8, total), F32),
            pltpu.VMEM((total, total), F32),
        ],
        compiler_params=params(),
        name="partial_gram",
    )(received)


def sum_kernel(blocks, panels, cores, sum_y, sum_x, count, in_ref, out_ref, mean_ref, between_ref, spread_ref):
    maps = 128
    parts = in_ref.shape[0]
    rows = in_ref.shape[1] - SIDE * panels
    per = rows // (panels * blocks)
    total_bins = float(count * parts)
    for m in range(panels):
        cols = slice(m * maps, (m + 1) * maps)
        mean_ref[:parts, cols] = jnp.concatenate(
            [in_ref[d, pl.ds(rows + m, 1), :] for d in range(parts)], axis=0
        )
        at = pl.ds(rows + 2 * panels + 2 * RIM * m, 2 * RIM)
        for y in range(sum_y):
            before = in_ref[(sum_x - 1) * sum_y + y, at, :]
            mean_ref[pl.ds(parts + 2 * RIM * y, 2 * RIM), cols] = before + in_ref[(y + 1) % sum_y, at, :]
    means = mean_ref[...]
    row = lax.broadcasted_iota(jnp.int32, (means.shape[0], 1), 0)
    weight = jnp.where(row < parts, float(count), 1.0)
    weight = jnp.where((row < parts) & (row >= parts - sum_y), float(count - 2 * RIM), weight)
    dev = means - jnp.sum(means * weight, axis=0, keepdims=True) * (1.0 / total_bins)
    own = jnp.concatenate(
        [
            sum(in_ref[d, pl.ds(rows + panels + m, 1), :] for d in range(parts))
            for m in range(panels)
        ],
        axis=1,
    )
    spread = (own + jnp.sum(dev * dev * weight, axis=0, keepdims=True)) * (1.0 / total_bins)
    y = lax.axis_index("y")
    x = lax.axis_index("x")
    for m in range(panels):

        @pl.when(y == m)
        def _():
            cols = slice(m * maps, (m + 1) * maps)
            between_ref[...] = dot_tn(dev[:, cols] * weight, dev)
            spread_ref[...] = jnp.transpose(jnp.broadcast_to(spread[:, cols], (maps, maps)))

    for z in range(blocks):
        start = pl.multiple_of((z * sum_x + x) * per, per)
        between = between_ref[pl.ds(start, per), :]
        spread_q = spread_ref[pl.ds(start, per), :]
        for m in range(panels):
            tile = pl.ds((m * blocks + z) * per, per)
            acc = in_ref[0, tile, :]
            for d in range(1, parts):
                acc = acc + in_ref[d, tile, :]
            cols = slice(m * maps, (m + 1) * maps)
            dest = place(z, m, blocks, cores)
            out_ref[dest, pl.ds(0, per), :] = (acc + between[:, cols]) * (1.0 / total_bins)
            out_ref[dest, pl.ds(per, per), :] = jnp.sqrt(spread_q * spread[:, cols])


def summed(received, blocks, panels, cores, sum_y, sum_x, count):
    parts = received.shape[0]
    per = (received.shape[1] - SIDE * panels) // (panels * blocks)
    vmem = pl.BlockSpec(memory_space=pltpu.VMEM)
    return pl.pallas_call(
        lambda *refs: sum_kernel(blocks, panels, cores, sum_y, sum_x, count, *refs),
        in_specs=[vmem],
        out_specs=vmem,
        out_shape=jax.ShapeDtypeStruct((blocks * panels, 2 * per, 128), F32),
        scratch_shapes=[
            pltpu.VMEM((parts + 2 * RIM * sum_y, panels * 128), F32),
            pltpu.VMEM((128, panels * 128), F32),
            pltpu.VMEM((128, 128), F32),
        ],
        compiler_params=params(),
        name="sum_parts",
    )(received)


def final_kernel(in_ref, gram_ref, scc_ref):
    strata, rows, _ = in_ref.shape
    per = rows // 2
    top = jnp.zeros((per, 128), F32)
    bottom = jnp.zeros((per, 128), F32)
    for k in range(strata):
        tile = in_ref[k, pl.ds(0, per), :]
        gram_ref[:, k, :] = tile
        top = top + tile
        bottom = bottom + in_ref[k, pl.ds(per, per), :]
    scc_ref[...] = top / bottom


def final(received):
    strata, rows, lanes = received.shape
    vmem = pl.BlockSpec(memory_space=pltpu.VMEM)
    return pl.pallas_call(
        final_kernel,
        in_specs=[vmem],
        out_specs=[vmem, vmem],
        out_shape=[
            jax.ShapeDtypeStruct((rows // 2, strata, lanes), F32),
            jax.ShapeDtypeStruct((rows // 2, lanes), F32),
        ],
        compiler_params=params(),
        name="final",
    )(received)


def body(band_maps, stratum_ids, half_width):
    maps, wide, bins = band_maps.shape
    blocks, sum_y, sum_x = (lax.axis_size(a) for a in ("zl", "y", "x"))
    panels = lax.axis_size(MAPS_AXES)
    cores = lax.axis_size("core")
    edge, band_maps = edges(pltpu.with_memory_space_constraint(band_maps, pltpu.HBM))
    ahead = lax.ppermute(edge, HALO_AXES, next_to_here())
    ready = inner(band_maps, stratum_ids, half_width)
    strata = smoothed(*ready, ahead, stratum_ids, half_width)
    strata = lax.all_to_all(strata, STRATA_AXES, 0, 0, tiled=True)
    parts = partial_gram(strata, blocks, panels, cores, sum_y, sum_x)
    parts = lax.all_to_all(parts, SUM_AXES, 0, 0, tiled=True)
    tiles = summed(parts, blocks, panels, cores, sum_y, sum_x, blocks * bins)
    tiles = lax.all_to_all(tiles, STRATA_AXES, 0, 0, tiled=True)
    gram, scc = final(tiles)
    return gram, scc


def solution(mesh):
    split = Mesh(mesh.devices.reshape(4, 4, 4, 2, 2), BINS_AXES + MAPS_AXES)
    in_specs = (P(MAPS_AXES, None, BINS_AXES), P(), P())
    out_specs = (P(BINS_AXES, None, MAPS_AXES), P(BINS_AXES, MAPS_AXES))
    return jax.shard_map(body, mesh=split, in_specs=in_specs, out_specs=out_specs, check_vma=False)
```

```python
import jax
import jax.numpy as jnp
from jax import lax
from jax.experimental import pallas as pl
from jax.experimental.pallas import tpu as pltpu
from jax.sharding import Mesh, PartitionSpec as P

HMAX = 2
X_AXES = ("xh", "xl")
BINS_AXES = ("y", "zl") + X_AXES
MAPS_AXES = ("zh", "core")
HALO_AXES = BINS_AXES + ("zh",)
STRATA_AXES = ("zh", "zl", "xl")
SUM_AXES = ("xh", "y")
F32 = jnp.float32
BF16 = jnp.bfloat16
HALO = 4
TAIL = 8
RIM = 2
SIDE = 64
SPAN = 200.0
VMEM_LIMIT = 28 * 1024 * 1024


def place(zh, zl, xl, blocks, pairs):
    return (zh * blocks + zl) * pairs + xl


def next_to_here():
    zl, x, zh = (lax.axis_size(a) for a in ("zl", X_AXES, "zh"))
    pairs = []
    for y in range(lax.axis_size("y")):
        flat = [((y * zl + p // x % zl) * x + p % x) * zh + p // (x * zl) for p in range(zh * zl * x)]
        pairs += [(flat[(p + 1) % len(flat)], flat[p]) for p in range(len(flat))]
    return pairs


def params():
    return pltpu.CompilerParams(vmem_limit_bytes=VMEM_LIMIT)


def edge_kernel(band_ref, edge_ref, copy_ref, sems):
    maps, wide, bins = band_ref.shape
    copies = [
        pltpu.make_async_copy(band_ref.at[:, :, lanes], copy_ref.at[:, :, lanes], sems.at[half])
        for half, lanes in enumerate((pl.ds(0, 128), pl.ds(128, bins - 128)))
    ]
    for copy in copies:
        copy.start()
    column = lax.broadcasted_iota(jnp.int32, (128, 128), 0)
    part = lax.rem(lax.broadcasted_iota(jnp.int32, (128, 128), 1), HALO)
    pick = (column == part).astype(BF16)
    offset = lax.broadcasted_iota(jnp.int32, (wide, 128), 0)
    lane = lax.broadcasted_iota(jnp.int32, (wide, 128), 1)
    own = (lax.div(lane, HALO) == offset)[None]
    copies[0].wait()
    data = copy_ref[:, :, pl.ds(0, 128)].reshape(maps * wide, 128)
    spread = jnp.dot(data, pick, preferred_element_type=F32).reshape(maps, wide, 128)
    edge_ref[...] = jnp.sum(jnp.where(own, spread, 0.0), axis=1).astype(BF16)
    copies[1].wait()


def edges(band_maps):
    maps, wide, bins = band_maps.shape
    vmem = pl.BlockSpec(memory_space=pltpu.VMEM)
    return pl.pallas_call(
        edge_kernel,
        in_specs=[pl.BlockSpec(memory_space=pltpu.HBM)],
        out_specs=[vmem, vmem],
        out_shape=[
            jax.ShapeDtypeStruct((maps, 128), BF16),
            jax.ShapeDtypeStruct(band_maps.shape, BF16),
        ],
        scratch_shapes=[pltpu.SemaphoreType.DMA((2,))],
        compiler_params=params(),
        cost_estimate=pl.CostEstimate(flops=2 * maps * wide * 128 * 128, bytes_accessed=2**22, transcendentals=0),
        name="edges",
    )(band_maps)


def windows(planes, win_ref, rows):
    wide = len(planes)
    for mid in range(1, wide - 1):
        one = planes[mid - 1] + planes[mid] + planes[mid + 1]
        win_ref[0, mid, rows, :] = one
        if 2 <= mid < wide - 2:
            win_ref[1, mid, rows, :] = one + (planes[mid - 2] + planes[mid + 2])


def box_of(win_ref, wider, centre):
    h = jnp.where(wider, 1, 0)
    reach = jnp.where(wider, 2, 0)
    outer = jnp.where(wider, 1.0, 0.0)
    scale = jnp.where(wider, 1.0 / 25.0, 1.0 / 9.0)

    def box(at, size):
        acc = win_ref[h, centre, pl.ds(at, size), :]
        acc = acc + win_ref[h, centre + 1, pl.ds(at - 1, size), :]
        acc = acc + win_ref[h, centre - 1, pl.ds(at + 1, size), :]
        far = win_ref[h, centre + reach, pl.ds(at - 2, size), :]
        far = far + win_ref[h, centre - reach, pl.ds(at + 2, size), :]
        return (acc + far * outer) * scale

    return box


def inner_kernel(
    ids_ref, half_ref, band_ref, sums_ref, total_ref, first_win_ref, last_win_ref, plane_ref, turned_ref, win_ref, perm_ref
):
    maps, wide, bins = band_ref.shape
    strata = sums_ref.shape[0]
    r = lax.broadcasted_iota(jnp.int32, (8 * wide, 8 * wide), 0)
    c = lax.broadcasted_iota(jnp.int32, (8 * wide, 8 * wide), 1)
    perm_ref[...] = (c == lax.rem(r, 8) * wide + lax.div(r, 8)).astype(BF16)
    for g in range(maps // 8):
        group = jnp.dot(
            perm_ref[...], band_ref[pl.ds(8 * g, 8)].reshape(8 * wide, bins), preferred_element_type=F32
        )
        plane_ref[:, pl.ds(8 * g, 8), :] = group.reshape(wide, 8, bins)

    def turn(d, carry):
        for half in range(bins // 128):
            tile = plane_ref[d, :, half * 128 : half * 128 + 128]
            turned_ref[d, pl.ds(half * 128, 128), :] = jnp.transpose(tile)
        return carry

    lax.fori_loop(0, wide, turn, 0, unroll=4)

    def some(i, carry):
        rows = pl.ds(pl.multiple_of(i * 16, 16), 16)
        windows([turned_ref[d, rows, :] for d in range(wide)], win_ref, rows)
        return carry

    lax.fori_loop(0, bins // 16, some, 0)
    first_win_ref[...] = win_ref[:, :, pl.ds(0, 8), :]
    last_win_ref[...] = win_ref[:, :, pl.ds(bins - 8, 8), :]

    def stratum(k, carry):
        box = box_of(win_ref, half_ref[k] >= 2, ids_ref[k])
        total = jnp.zeros((1, maps), F32)
        for at in range(0, bins - TAIL, 64):
            size = min(64, bins - TAIL - at)
            part = box(at + 2, size)
            sums_ref[k, pl.ds(at, size), :] = part
            total = total + jnp.sum(part, axis=0, keepdims=True)
        total_ref[k] = jnp.broadcast_to(total, (8, maps))
        return carry

    lax.fori_loop(0, strata, stratum, 0, unroll=2)


def inner(band_maps, stratum_ids, half_width):
    maps, wide, bins = band_maps.shape
    strata = stratum_ids.shape[0]
    smem = pl.BlockSpec(memory_space=pltpu.SMEM)
    vmem = pl.BlockSpec(memory_space=pltpu.VMEM)
    return pl.pallas_call(
        inner_kernel,
        in_specs=[smem, smem, vmem],
        out_specs=[vmem, vmem, vmem, vmem],
        out_shape=[
            jax.ShapeDtypeStruct((strata, bins - TAIL, maps), F32),
            jax.ShapeDtypeStruct((strata, 8, maps), F32),
            jax.ShapeDtypeStruct((2, wide, 8, maps), F32),
            jax.ShapeDtypeStruct((2, wide, 8, maps), F32),
        ],
        scratch_shapes=[
            pltpu.VMEM((wide, maps, bins), F32),
            pltpu.VMEM((wide, bins, maps), F32),
            pltpu.VMEM((2, wide, bins, maps), F32),
            pltpu.VMEM((8 * wide, 8 * wide), BF16),
        ],
        compiler_params=params(),
        cost_estimate=pl.CostEstimate(flops=2 * maps * wide * bins * 256, bytes_accessed=2**22, transcendentals=0),
        name="inner",
    )(stratum_ids, half_width, band_maps)


def words_of(value):
    hi = value.astype(BF16).astype(F32)
    mid = (value - hi).astype(BF16).astype(F32)
    return hi, mid, value - hi - mid


def smooth_kernel(
    ids_ref, half_ref, sums_ref, total_ref, first_win_ref, last_win_ref, next_ref, out_ref, win_ref, start_ref
):
    strata, ready, maps = sums_ref.shape
    wide = first_win_ref.shape[1]
    bins = ready + TAIL
    y, z, x = (lax.axis_index(a) for a in ("y", "zl", X_AXES))
    last_y, last_z, last_x = (lax.axis_size(a) - 1 for a in ("y", "zl", X_AXES))
    before = (z == last_z) & (x == last_x)
    after = (z == 0) & (x == 0)
    ahead = jnp.where(before, 0.0, jnp.transpose(next_ref[...].astype(F32)))
    row8 = lax.broadcasted_iota(jnp.int32, (8, maps), 0)
    tails = []
    for d in range(wide):
        at = HALO * d
        tile = pltpu.roll(ahead[at // 8 * 8 : at // 8 * 8 + 8], (-(at % 8)) % 8, axis=0)
        tails.append(jnp.where(row8 < HALO, tile, 0.0))
    win_ref[:, :, pl.ds(0, 8), :] = last_win_ref[...]
    windows(tails, win_ref, pl.ds(8, 8))
    start_ref[:, :, pl.ds(0, 8), :] = jnp.zeros((2, wide, 8, maps), F32)
    start_ref[:, :, pl.ds(8, 8), :] = first_win_ref[...]

    row = lax.broadcasted_iota(jnp.int32, (16, maps), 0)
    empty = before & (row8 >= 8 - 2 * RIM)
    seam_before = before & (row8 < 2 * RIM) & ((y < last_y) | (row8 < RIM))
    seam_after = after & (row8 < 2 * RIM) & ((y > 0) | (row8 >= RIM))
    per_slot = jnp.where(before, 1.0 / (bins - 2 * RIM), 1.0 / bins)

    def stratum(k, carry):
        wider, centre = half_ref[k] >= 2, ids_ref[k]
        end = box_of(win_ref, wider, centre)(2, 8)
        total = total_ref[k][:1] + jnp.sum(jnp.where(empty, 0.0, end), axis=0, keepdims=True)
        mean = total * per_slot
        square = jnp.zeros((1, maps), F32)
        for at in range(0, bins, 64):
            size = min(64, ready - at)
            part = sums_ref[k, pl.ds(at, size), :]
            if size < 64:
                part = jnp.concatenate([part, jnp.where(empty, mean, end)], axis=0)
            part = part - mean
            square = square + jnp.sum(part * part, axis=0, keepdims=True)
            out_ref[k, pl.ds(at, 64), :] = part.astype(BF16)
        seam = jnp.where(seam_before, pltpu.roll(end, 2 * RIM, axis=0), 0.0)
        seam = seam + jnp.where(seam_after, box_of(start_ref, wider, centre)(8 - RIM, 8), 0.0)
        side = jnp.zeros((16, maps), F32)
        for i, value in enumerate(words_of(mean) + words_of(square)):
            side = jnp.where(row == i, value, side)
        for i, value in enumerate(words_of(seam)[:2]):
            value = jnp.concatenate([value, jnp.zeros((8, maps), F32)], axis=0)
            side = side + pltpu.roll(value, 6 + 2 * RIM * i, axis=0)
        out_ref[k, pl.ds(bins, 16), :] = side.astype(BF16)
        return carry

    lax.fori_loop(0, strata, stratum, 0, unroll=2)


def smoothed(sums, total, first_win, last_win, ahead, stratum_ids, half_width):
    strata, ready, maps = sums.shape
    wide = first_win.shape[1]
    smem = pl.BlockSpec(memory_space=pltpu.SMEM)
    vmem = pl.BlockSpec(memory_space=pltpu.VMEM)
    return pl.pallas_call(
        smooth_kernel,
        in_specs=[smem, smem] + [vmem] * 5,
        out_specs=vmem,
        out_shape=jax.ShapeDtypeStruct((strata, ready + TAIL + 16, maps), BF16),
        scratch_shapes=[
            pltpu.VMEM((2, wide, 16, maps), F32),
            pltpu.VMEM((2, wide, 16, maps), F32),
        ],
        compiler_params=params(),
        name="smooth",
    )(stratum_ids, half_width, sums, total, first_win, last_win, ahead)


def encode(r):
    size = jnp.exp2(jnp.abs(r) * SPAN - 0.5 * SPAN)
    return jnp.where(r < 0.0, -size, size)


def decode(code):
    size = jnp.log2(jnp.abs(code)) * (1.0 / SPAN) + 0.5
    return jnp.where(code < 0.0, -size, size)


def dot_tn(a, b):
    return lax.dot_general(
        a, b, (((0,), (0,)), ((), ())), precision=lax.Precision.HIGHEST, preferred_element_type=F32
    )


def gram_kernel(blocks, halves, pairs, sum_y, sum_x, bins, own_ref, other_ref, out_ref, data_ref, mean_ref, gram_ref):
    maps = 128
    panels = 2 * halves
    total = panels * maps
    mine = halves * maps
    count_blocks = blocks * pairs
    squares, seams = [], []
    for m in range(panels):
        in_ref = (own_ref, other_ref)[m // halves]
        square, seam = [], []
        for z in range(blocks):
            for x in range(pairs):
                src = place(m % halves, z, x, blocks, pairs)
                b = z * pairs + x
                data_ref[pl.ds(b * bins, bins), pl.ds(m * maps, maps)] = in_ref[src, pl.ds(0, bins), :]
                words = in_ref[src, pl.ds(bins, 16), :].astype(F32)
                mean_ref[b : b + 1, m * maps : (m + 1) * maps] = words[0:1] + words[1:2] + words[2:3]
                square.append(words[3:4] + words[4:5] + words[5:6])
                seam.append(words[6:10] + words[10:14])
        squares.append(sum(square))
        seams.append(sum(seam))
    means = mean_ref[...]
    short = lax.axis_index("xh") == sum_x - 1
    b = lax.broadcasted_iota(jnp.int32, (count_blocks, 1), 0)
    count = jnp.where(short & (b == count_blocks - 1), float(bins - 2 * RIM), float(bins))
    centre = jnp.sum(means * count, axis=0, keepdims=True)
    centre = centre * jnp.where(short, 1.0 / (count_blocks * bins - 2 * RIM), 1.0 / (count_blocks * bins))
    dev = means - centre
    hi, mid, low = words_of(dev[:, :mine])
    left_hi, left_mid, left_low = words_of(dev * count)
    pad = -6 * count_blocks % 32
    left = [left_hi, left_hi, left_mid, left_mid, left_hi, left_low, jnp.zeros((pad, total), F32)]
    right = [hi, mid, hi, mid, low, hi, jnp.zeros((pad, mine), F32)]
    left, right = (jnp.concatenate(a, axis=0).astype(BF16) for a in (left, right))
    tn = (((0,), (0,)), ((), ()))
    gram_ref[...] = lax.dot_general(
        data_ref[...], data_ref[:, :mine], tn, preferred_element_type=F32
    ) + lax.dot_general(left, right, tn, preferred_element_type=F32)
    squares = jnp.concatenate(squares, axis=1) + jnp.sum(dev * dev * count, axis=0, keepdims=True)
    by_lane = jnp.where(squares > 0.0, lax.rsqrt(squares), 0.0)

    def rows_of(line):
        return jnp.concatenate([line[:, m * maps : (m + 1) * maps] for m in range(panels)], axis=0)

    side = words_of(rows_of(centre)) + words_of(rows_of(squares)) + words_of(jnp.concatenate(seams, axis=0))[:2]
    side += (jnp.zeros((SIDE - (6 + 4 * RIM) * panels, maps), F32),)
    side = jnp.concatenate(side, axis=0).astype(BF16)
    core = lax.axis_index("core")
    per = maps // (blocks * sum_x)
    for q in range(panels):
        y = (q % halves) * 2 + (core if q < halves else 1 - core)
        by_row = jnp.transpose(jnp.broadcast_to(by_lane[:, q * maps : (q + 1) * maps], (maps, maps)))
        for m in range(halves):
            cols = slice(m * maps, (m + 1) * maps)
            code = encode(gram_ref[pl.ds(q * maps, maps), cols] * by_row * by_lane[:, cols]).astype(BF16)
            for x in range(sum_x):
                for z in range(blocks):
                    at = (z * sum_x + x) * per
                    out_ref[x * sum_y + y, pl.ds((m * blocks + z) * per, per), :] = code[at : at + per]
    for d in range(sum_x * sum_y):
        out_ref[d, pl.ds(halves * blocks * per, SIDE), :] = side


def partial_gram(own, other, blocks, halves, pairs, sum_y, sum_x):
    bins = own.shape[1] - 16
    total = 2 * halves * 128
    per = 128 // (blocks * sum_x)
    vmem = pl.BlockSpec(memory_space=pltpu.VMEM)
    return pl.pallas_call(
        lambda *refs: gram_kernel(blocks, halves, pairs, sum_y, sum_x, bins, *refs),
        in_specs=[vmem, vmem],
        out_specs=vmem,
        out_shape=jax.ShapeDtypeStruct((sum_y * sum_x, halves * blocks * per + SIDE, 128), BF16),
        scratch_shapes=[
            pltpu.VMEM((blocks * pairs * bins, total), BF16),
            pltpu.VMEM((blocks * pairs, total), F32),
            pltpu.VMEM((total, total // 2), F32),
        ],
        compiler_params=params(),
        name="partial_gram",
    )(own, other)


def sum_kernel(
    blocks, halves, pairs, sum_y, sum_x, count, in_ref, out_ref, mean_ref, scale_ref, between_ref, spread_ref, column_ref
):
    maps = 128
    panels = 2 * halves
    parts = in_ref.shape[0]
    rows = in_ref.shape[1] - SIDE
    per = rows // (halves * blocks)
    tile = per // pairs
    total_bins = float(count * parts)
    squares = jnp.zeros((panels, maps), F32)
    seams = []
    for d in range(parts):
        side = in_ref[d, pl.ds(rows, SIDE), :].astype(F32)
        mean, square = (
            side[i : i + panels] + side[i + panels : i + 2 * panels] + side[i + 2 * panels : i + 3 * panels]
            for i in (0, 3 * panels)
        )
        size = 2 * RIM * panels
        seams.append(side[6 * panels : 6 * panels + size] + side[6 * panels + size : 6 * panels + 2 * size])
        squares = squares + square
        scale = jnp.sqrt(square)
        for m in range(panels):
            mean_ref[d : d + 1, m * maps : (m + 1) * maps] = mean[m : m + 1]
            scale_ref[d : d + 1, m * maps : (m + 1) * maps] = scale[m : m + 1]
    for y in range(sum_y):
        seam = seams[(sum_x - 1) * sum_y + y] + seams[(y + 1) % sum_y]
        for m in range(panels):
            mean_ref[pl.ds(parts + 2 * RIM * y, 2 * RIM), m * maps : (m + 1) * maps] = seam[
                2 * RIM * m : 2 * RIM * (m + 1)
            ]
    means = mean_ref[...]
    row = lax.broadcasted_iota(jnp.int32, (means.shape[0], 1), 0)
    weight = jnp.where(row < parts, float(count), 1.0)
    weight = jnp.where((row < parts) & (row >= parts - sum_y), float(count - 2 * RIM), weight)
    dev = means - jnp.sum(means * weight, axis=0, keepdims=True) * (1.0 / total_bins)
    own = jnp.concatenate([squares[m : m + 1] for m in range(panels)], axis=1)
    spread = (own + jnp.sum(dev * dev * weight, axis=0, keepdims=True)) * (1.0 / total_bins)
    scales = scale_ref[...]
    y = lax.axis_index("y")
    x = lax.axis_index("xh")
    rows_panel = y // 2 + jnp.where(y % 2 == lax.axis_index("core"), 0, halves)
    for m in range(panels):

        @pl.when(rows_panel == m)
        def _():
            cols = slice(m * maps, (m + 1) * maps)
            between_ref[...] = dot_tn(dev[:, cols] * weight, dev[:, : halves * maps])
            spread_ref[...] = jnp.transpose(jnp.broadcast_to(spread[:, cols], (maps, maps)))
            column = jnp.concatenate([scales[:, cols], jnp.zeros((maps - parts, maps), F32)], axis=0)
            column_ref[...] = jnp.transpose(column)

    for z in range(blocks):
        spot = pl.ds(pl.multiple_of((z * sum_x + x) * per, per), per)
        column = column_ref[spot, :]
        acc = [between_ref[spot, m * maps : (m + 1) * maps] for m in range(halves)]
        for d in range(parts):
            by_row = jnp.broadcast_to(column[:, d : d + 1], (per, maps))
            for m in range(halves):
                code = in_ref[d, pl.ds((m * blocks + z) * per, per), :].astype(F32)
                by_lane = scales[d : d + 1, m * maps : (m + 1) * maps]
                acc[m] = acc[m] + decode(code) * by_row * by_lane
        for m in range(halves):
            bottom = jnp.sqrt(spread_ref[spot, :] * spread[:, m * maps : (m + 1) * maps])
            for j in range(pairs):
                dest = place(m, z, j, blocks, pairs)
                part = slice(j * tile, (j + 1) * tile)
                out_ref[dest, pl.ds(0, tile), :] = acc[m][part] * (1.0 / total_bins)
                out_ref[dest, pl.ds(tile, tile), :] = bottom[part]


def summed(received, blocks, halves, pairs, sum_y, sum_x, count):
    parts = received.shape[0]
    tile = (received.shape[1] - SIDE) // (halves * blocks * pairs)
    total = 2 * halves * 128
    vmem = pl.BlockSpec(memory_space=pltpu.VMEM)
    return pl.pallas_call(
        lambda *refs: sum_kernel(blocks, halves, pairs, sum_y, sum_x, count, *refs),
        in_specs=[vmem],
        out_specs=vmem,
        out_shape=jax.ShapeDtypeStruct((halves * blocks * pairs, 2 * tile, 128), F32),
        scratch_shapes=[
            pltpu.VMEM((parts + 2 * RIM * sum_y, total), F32),
            pltpu.VMEM((parts, total), F32),
            pltpu.VMEM((128, total // 2), F32),
            pltpu.VMEM((128, 128), F32),
            pltpu.VMEM((128, 128), F32),
        ],
        compiler_params=params(),
        name="sum_parts",
    )(received)


def final_kernel(in_ref, gram_ref, scc_ref):
    strata, rows, _ = in_ref.shape
    per = rows // 2
    top = jnp.zeros((per, 128), F32)
    bottom = jnp.zeros((per, 128), F32)
    for k in range(strata):
        tile = in_ref[k, pl.ds(0, per), :]
        gram_ref[:, k, :] = tile
        top = top + tile
        bottom = bottom + in_ref[k, pl.ds(per, per), :]
    scc_ref[...] = top / bottom


def final(received):
    strata, rows, lanes = received.shape
    vmem = pl.BlockSpec(memory_space=pltpu.VMEM)
    return pl.pallas_call(
        final_kernel,
        in_specs=[vmem],
        out_specs=[vmem, vmem],
        out_shape=[
            jax.ShapeDtypeStruct((rows // 2, strata, lanes), F32),
            jax.ShapeDtypeStruct((rows // 2, lanes), F32),
        ],
        compiler_params=params(),
        name="final",
    )(received)


def body(band_maps, stratum_ids, half_width):
    maps, wide, bins = band_maps.shape
    blocks, halves, pairs, sum_y, sum_x = (lax.axis_size(a) for a in ("zl", "zh", "xl", "y", "xh"))
    edge, band_maps = edges(pltpu.with_memory_space_constraint(band_maps, pltpu.HBM))
    ahead = lax.ppermute(edge, HALO_AXES, next_to_here())
    ready = inner(band_maps, stratum_ids, half_width)
    strata = smoothed(*ready, ahead, stratum_ids, half_width)
    strata = lax.all_to_all(strata, STRATA_AXES, 0, 0, tiled=True)
    other = lax.ppermute(strata, "core", [(0, 1), (1, 0)])
    parts = partial_gram(strata, other, blocks, halves, pairs, sum_y, sum_x)
    parts = lax.all_to_all(parts, SUM_AXES, 0, 0, tiled=True)
    tiles = summed(parts, blocks, halves, pairs, sum_y, sum_x, blocks * pairs * bins)
    tiles = lax.all_to_all(tiles, STRATA_AXES, 0, 0, tiled=True)
    gram, scc = final(tiles)
    return gram, scc


def solution(mesh):
    split = Mesh(mesh.devices.reshape(4, 4, 2, 2, 2, 2), BINS_AXES + MAPS_AXES)
    in_specs = (P(MAPS_AXES, None, BINS_AXES), P(), P())
    out_specs = (P(BINS_AXES, None, MAPS_AXES), P(BINS_AXES, MAPS_AXES))
    return jax.shard_map(body, mesh=split, in_specs=in_specs, out_specs=out_specs, check_vma=False)
```

```python
import jax
import jax.numpy as jnp
from jax import lax
from jax.experimental import pallas as pl
from jax.experimental.pallas import tpu as pltpu
from jax.sharding import Mesh, PartitionSpec as P

HMAX = 2
X_AXES = ("xh", "xl")
BINS_AXES = ("y", "zl") + X_AXES
MAPS_AXES = ("zh", "core")
HALO_AXES = BINS_AXES + ("zh",)
STRATA_AXES = ("zh", "zl", "xl")
SUM_AXES = ("xh", "y")
F32 = jnp.float32
BF16 = jnp.bfloat16
HALO = 4
HEAD = 8
RIM = 2
SIDE = 64
SPAN = 200.0
VMEM_LIMIT = 28 * 1024 * 1024


def place(zh, zl, xl, blocks, pairs):
    return (zh * blocks + zl) * pairs + xl


def to_next():
    zl, x, zh = (lax.axis_size(a) for a in ("zl", X_AXES, "zh"))
    pairs = []
    for y in range(lax.axis_size("y")):
        flat = [((y * zl + p // x % zl) * x + p % x) * zh + p // (x * zl) for p in range(zh * zl * x)]
        pairs += [(flat[p], flat[(p + 1) % len(flat)]) for p in range(len(flat))]
    return pairs


def params():
    return pltpu.CompilerParams(vmem_limit_bytes=VMEM_LIMIT)


def edge_kernel(band_ref, edge_ref, copy_ref, sems):
    maps, wide, bins = band_ref.shape
    copies = [
        pltpu.make_async_copy(band_ref.at[:, :, lanes], copy_ref.at[:, :, lanes], sems.at[half])
        for half, lanes in enumerate((pl.ds(bins - 128, 128), pl.ds(0, bins - 128)))
    ]
    for copy in copies:
        copy.start()
    column = lax.broadcasted_iota(jnp.int32, (128, 128), 0)
    part = lax.rem(lax.broadcasted_iota(jnp.int32, (128, 128), 1), HALO)
    pick = (column == 128 - HALO + part).astype(BF16)
    offset = lax.broadcasted_iota(jnp.int32, (wide, 128), 0)
    lane = lax.broadcasted_iota(jnp.int32, (wide, 128), 1)
    own = (lax.div(lane, HALO) == offset)[None]
    copies[0].wait()
    data = copy_ref[:, :, pl.ds(bins - 128, 128)].reshape(maps * wide, 128)
    spread = jnp.dot(data, pick, preferred_element_type=F32).reshape(maps, wide, 128)
    edge_ref[...] = jnp.sum(jnp.where(own, spread, 0.0), axis=1).astype(BF16)
    copies[1].wait()


def edges(band_maps):
    maps, wide, bins = band_maps.shape
    vmem = pl.BlockSpec(memory_space=pltpu.VMEM)
    return pl.pallas_call(
        edge_kernel,
        in_specs=[pl.BlockSpec(memory_space=pltpu.HBM)],
        out_specs=[vmem, vmem],
        out_shape=[
            jax.ShapeDtypeStruct((maps, 128), BF16),
            jax.ShapeDtypeStruct(band_maps.shape, BF16),
        ],
        scratch_shapes=[pltpu.SemaphoreType.DMA((2,))],
        compiler_params=params(),
        cost_estimate=pl.CostEstimate(flops=2 * maps * wide * 128 * 128, bytes_accessed=2**22, transcendentals=0),
        name="edges",
    )(band_maps)


def windows(planes, win_ref, rows):
    wide = len(planes)
    for mid in range(1, wide - 1):
        one = planes[mid - 1] + planes[mid] + planes[mid + 1]
        win_ref[0, mid, rows, :] = one
        if 2 <= mid < wide - 2:
            win_ref[1, mid, rows, :] = one + (planes[mid - 2] + planes[mid + 2])


def box_of(win_ref, wider, centre):
    h = jnp.where(wider, 1, 0)
    reach = jnp.where(wider, 2, 0)
    outer = jnp.where(wider, 1.0, 0.0)
    scale = jnp.where(wider, 1.0 / 25.0, 1.0 / 9.0)

    def box(at, size):
        acc = win_ref[h, centre, pl.ds(at, size), :]
        acc = acc + win_ref[h, centre + 1, pl.ds(at - 1, size), :]
        acc = acc + win_ref[h, centre - 1, pl.ds(at + 1, size), :]
        far = win_ref[h, centre + reach, pl.ds(at - 2, size), :]
        far = far + win_ref[h, centre - reach, pl.ds(at + 2, size), :]
        return (acc + far * outer) * scale

    return box


def inner_kernel(
    ids_ref, half_ref, band_ref, sums_ref, total_ref, first_win_ref, last_win_ref, plane_ref, turned_ref, win_ref, perm_ref
):
    maps, wide, bins = band_ref.shape
    strata = sums_ref.shape[0]
    r = lax.broadcasted_iota(jnp.int32, (8 * wide, 8 * wide), 0)
    c = lax.broadcasted_iota(jnp.int32, (8 * wide, 8 * wide), 1)
    perm_ref[...] = (c == lax.rem(r, 8) * wide + lax.div(r, 8)).astype(BF16)
    for g in range(0, maps, 16):
        pair = [
            jnp.dot(
                perm_ref[...], band_ref[pl.ds(g + 8 * j, 8)].reshape(8 * wide, bins), preferred_element_type=F32
            ).reshape(wide, 8, bins)
            for j in range(2)
        ]
        plane_ref[:, pl.ds(g, 16), :] = jnp.concatenate(pair, axis=1).astype(BF16)

    for d in range(wide):
        for half in range(bins // 128):
            tile = plane_ref[d, :, half * 128 : half * 128 + 128]
            turned_ref[d, pl.ds(half * 128, 128), :] = jnp.transpose(tile).astype(F32)

    def some(i, carry):
        rows = pl.ds(pl.multiple_of(i * 16, 16), 16)
        windows([turned_ref[d, rows, :] for d in range(wide)], win_ref, rows)
        return carry

    lax.fori_loop(0, bins // 16, some, 0)
    first_win_ref[...] = win_ref[:, :, pl.ds(0, 8), :]
    last_win_ref[...] = win_ref[:, :, pl.ds(bins - 8, 8), :]

    def stratum(k, carry):
        box = box_of(win_ref, half_ref[k] >= 2, ids_ref[k])
        total = jnp.zeros((1, maps), F32)
        for at in range(0, bins - HEAD, 64):
            size = min(64, bins - HEAD - at)
            part = box(at + HEAD - RIM, size)
            sums_ref[k, pl.ds(at, size), :] = part
            total = total + jnp.sum(part, axis=0, keepdims=True)
        total_ref[k] = jnp.broadcast_to(total, (8, maps))
        return carry

    lax.fori_loop(0, strata, stratum, 0, unroll=4)


def inner(band_maps, stratum_ids, half_width):
    maps, wide, bins = band_maps.shape
    strata = stratum_ids.shape[0]
    smem = pl.BlockSpec(memory_space=pltpu.SMEM)
    vmem = pl.BlockSpec(memory_space=pltpu.VMEM)
    return pl.pallas_call(
        inner_kernel,
        in_specs=[smem, smem, vmem],
        out_specs=[vmem, vmem, vmem, vmem],
        out_shape=[
            jax.ShapeDtypeStruct((strata, bins - HEAD, maps), F32),
            jax.ShapeDtypeStruct((strata, 8, maps), F32),
            jax.ShapeDtypeStruct((2, wide, 8, maps), F32),
            jax.ShapeDtypeStruct((2, wide, 8, maps), F32),
        ],
        scratch_shapes=[
            pltpu.VMEM((wide, maps, bins), BF16),
            pltpu.VMEM((wide, bins, maps), F32),
            pltpu.VMEM((2, wide, bins, maps), F32),
            pltpu.VMEM((8 * wide, 8 * wide), BF16),
        ],
        compiler_params=params(),
        cost_estimate=pl.CostEstimate(flops=2 * maps * wide * bins * 256, bytes_accessed=2**22, transcendentals=0),
        name="inner",
    )(stratum_ids, half_width, band_maps)


def words_of(value):
    hi = value.astype(BF16).astype(F32)
    mid = (value - hi).astype(BF16).astype(F32)
    return hi, mid, value - hi - mid


def smooth_kernel(
    ids_ref, half_ref, sums_ref, total_ref, first_win_ref, last_win_ref, behind_ref, out_ref, start_ref, stop_ref
):
    strata, ready, maps = sums_ref.shape
    wide = first_win_ref.shape[1]
    bins = ready + HEAD
    y, z, x = (lax.axis_index(a) for a in ("y", "zl", X_AXES))
    last_y, last_z, last_x = (lax.axis_size(a) - 1 for a in ("y", "zl", X_AXES))
    before = (z == last_z) & (x == last_x)
    after = (z == 0) & (x == 0)
    behind = jnp.where(after, 0.0, jnp.transpose(behind_ref[...].astype(F32)))
    row8 = lax.broadcasted_iota(jnp.int32, (8, maps), 0)
    heads = []
    for d in range(wide):
        at = HALO * d
        tile = pltpu.roll(behind[at // 8 * 8 : at // 8 * 8 + 8], (8 - HALO - at % 8) % 8, axis=0)
        heads.append(jnp.where(row8 >= 8 - HALO, tile, 0.0))
    windows(heads, start_ref, pl.ds(0, 8))
    start_ref[:, :, pl.ds(8, 8), :] = first_win_ref[...]
    stop_ref[:, :, pl.ds(0, 8), :] = last_win_ref[...]
    stop_ref[:, :, pl.ds(8, 8), :] = jnp.zeros((2, wide, 8, maps), F32)

    row = lax.broadcasted_iota(jnp.int32, (16, maps), 0)
    empty = after & (row8 < 2 * RIM)
    seam_before = before & (row8 < 2 * RIM) & ((y < last_y) | (row8 < RIM))
    seam_after = after & (row8 < 2 * RIM) & ((y > 0) | (row8 >= RIM))
    per_slot = jnp.where(after, 1.0 / (bins - 2 * RIM), 1.0 / bins)

    def stratum(k, carry):
        wider, centre = half_ref[k] >= 2, ids_ref[k]
        head = box_of(start_ref, wider, centre)(8 - RIM, 8)
        total = total_ref[k][:1] + jnp.sum(jnp.where(empty, 0.0, head), axis=0, keepdims=True)
        mean = total * per_slot
        square = jnp.zeros((1, maps), F32)
        for at in range(0, bins, 64):
            if at == 0:
                part = [jnp.where(empty, mean, head), sums_ref[k, pl.ds(0, 64 - HEAD), :]]
                part = jnp.concatenate(part, axis=0)
            else:
                part = sums_ref[k, pl.ds(at - HEAD, 64), :]
            part = part - mean
            square = square + jnp.sum(part * part, axis=0, keepdims=True)
            out_ref[k, pl.ds(at, 64), :] = part.astype(BF16)
        seam = jnp.where(seam_before, box_of(stop_ref, wider, centre)(8 - RIM, 8), 0.0)
        seam = seam + jnp.where(seam_after, head, 0.0)
        side = jnp.zeros((16, maps), F32)
        for i, value in enumerate(words_of(mean) + words_of(square)):
            side = jnp.where(row == i, value, side)
        for i, value in enumerate(words_of(seam)[:2]):
            value = jnp.concatenate([value, jnp.zeros((8, maps), F32)], axis=0)
            side = side + pltpu.roll(value, 6 + 2 * RIM * i, axis=0)
        out_ref[k, pl.ds(bins, 16), :] = side.astype(BF16)
        return carry

    lax.fori_loop(0, strata, stratum, 0, unroll=2)


def smoothed(sums, total, first_win, last_win, behind, stratum_ids, half_width):
    strata, ready, maps = sums.shape
    wide = first_win.shape[1]
    smem = pl.BlockSpec(memory_space=pltpu.SMEM)
    vmem = pl.BlockSpec(memory_space=pltpu.VMEM)
    return pl.pallas_call(
        smooth_kernel,
        in_specs=[smem, smem] + [vmem] * 5,
        out_specs=vmem,
        out_shape=jax.ShapeDtypeStruct((strata, ready + HEAD + 16, maps), BF16),
        scratch_shapes=[
            pltpu.VMEM((2, wide, 16, maps), F32),
            pltpu.VMEM((2, wide, 16, maps), F32),
        ],
        compiler_params=params(),
        name="smooth",
    )(stratum_ids, half_width, sums, total, first_win, last_win, behind)


def encode(r):
    size = jnp.exp2(jnp.abs(r) * SPAN - 0.5 * SPAN)
    return jnp.where(r < 0.0, -size, size)


def decode(code):
    size = jnp.log2(jnp.abs(code)) * (1.0 / SPAN) + 0.5
    return jnp.where(code < 0.0, -size, size)


def dot_tn(a, b):
    return lax.dot_general(
        a, b, (((0,), (0,)), ((), ())), precision=lax.Precision.HIGHEST, preferred_element_type=F32
    )


def gram_kernel(blocks, halves, pairs, sum_y, sum_x, bins, own_ref, other_ref, out_ref, data_ref, mean_ref, gram_ref):
    maps = 128
    panels = 2 * halves
    total = panels * maps
    mine = halves * maps
    count_blocks = blocks * pairs
    squares, seams = [], []
    for m in range(panels):
        in_ref = (own_ref, other_ref)[m // halves]
        square, seam = [], []
        for z in range(blocks):
            for x in range(pairs):
                src = place(m % halves, z, x, blocks, pairs)
                b = z * pairs + x
                data_ref[pl.ds(b * bins, bins), pl.ds(m * maps, maps)] = in_ref[src, pl.ds(0, bins), :]
                words = in_ref[src, pl.ds(bins, 16), :].astype(F32)
                mean_ref[b : b + 1, m * maps : (m + 1) * maps] = words[0:1] + words[1:2] + words[2:3]
                square.append(words[3:4] + words[4:5] + words[5:6])
                seam.append(words[6:10] + words[10:14])
        squares.append(sum(square))
        seams.append(sum(seam))
    means = mean_ref[...]
    short = lax.axis_index("xh") == 0
    b = lax.broadcasted_iota(jnp.int32, (count_blocks, 1), 0)
    count = jnp.where(short & (b == 0), float(bins - 2 * RIM), float(bins))
    centre = jnp.sum(means * count, axis=0, keepdims=True)
    centre = centre * jnp.where(short, 1.0 / (count_blocks * bins - 2 * RIM), 1.0 / (count_blocks * bins))
    dev = means - centre
    hi, mid, low = words_of(dev[:, :mine])
    left_hi, left_mid, left_low = words_of(dev * count)
    pad = -6 * count_blocks % 32
    left = [left_hi, left_hi, left_mid, left_mid, left_hi, left_low, jnp.zeros((pad, total), F32)]
    right = [hi, mid, hi, mid, low, hi, jnp.zeros((pad, mine), F32)]
    left, right = (jnp.concatenate(a, axis=0).astype(BF16) for a in (left, right))
    tn = (((0,), (0,)), ((), ()))
    gram_ref[...] = lax.dot_general(
        data_ref[...], data_ref[:, :mine], tn, preferred_element_type=F32
    ) + lax.dot_general(left, right, tn, preferred_element_type=F32)
    squares = jnp.concatenate(squares, axis=1) + jnp.sum(dev * dev * count, axis=0, keepdims=True)
    by_lane = jnp.where(squares > 0.0, lax.rsqrt(squares), 0.0)

    def rows_of(line):
        return jnp.concatenate([line[:, m * maps : (m + 1) * maps] for m in range(panels)], axis=0)

    side = words_of(rows_of(centre)) + words_of(rows_of(squares)) + words_of(jnp.concatenate(seams, axis=0))[:2]
    side += (jnp.zeros((SIDE - (6 + 4 * RIM) * panels, maps), F32),)
    side = jnp.concatenate(side, axis=0).astype(BF16)
    core = lax.axis_index("core")
    per = maps // (blocks * sum_x)
    for q in range(panels):
        y = (q % halves) * 2 + (core if q < halves else 1 - core)
        by_row = jnp.transpose(jnp.broadcast_to(by_lane[:, q * maps : (q + 1) * maps], (maps, maps)))
        for m in range(halves):
            cols = slice(m * maps, (m + 1) * maps)
            code = encode(gram_ref[pl.ds(q * maps, maps), cols] * by_row * by_lane[:, cols]).astype(BF16)
            for x in range(sum_x):
                for z in range(blocks):
                    at = (z * sum_x + x) * per
                    out_ref[x * sum_y + y, pl.ds((m * blocks + z) * per, per), :] = code[at : at + per]
    for d in range(sum_x * sum_y):
        out_ref[d, pl.ds(halves * blocks * per, SIDE), :] = side


def partial_gram(own, other, blocks, halves, pairs, sum_y, sum_x):
    bins = own.shape[1] - 16
    total = 2 * halves * 128
    per = 128 // (blocks * sum_x)
    vmem = pl.BlockSpec(memory_space=pltpu.VMEM)
    return pl.pallas_call(
        lambda *refs: gram_kernel(blocks, halves, pairs, sum_y, sum_x, bins, *refs),
        in_specs=[vmem, vmem],
        out_specs=vmem,
        out_shape=jax.ShapeDtypeStruct((sum_y * sum_x, halves * blocks * per + SIDE, 128), BF16),
        scratch_shapes=[
            pltpu.VMEM((blocks * pairs * bins, total), BF16),
            pltpu.VMEM((blocks * pairs, total), F32),
            pltpu.VMEM((total, total // 2), F32),
        ],
        compiler_params=params(),
        name="partial_gram",
    )(own, other)


def sum_kernel(
    blocks, halves, pairs, sum_y, sum_x, count, in_ref, out_ref, mean_ref, scale_ref, between_ref, spread_ref, column_ref
):
    maps = 128
    panels = 2 * halves
    parts = in_ref.shape[0]
    rows = in_ref.shape[1] - SIDE
    per = rows // (halves * blocks)
    tile = per // pairs
    total_bins = float(count * parts)
    squares = jnp.zeros((panels, maps), F32)
    seams = []
    for d in range(parts):
        side = in_ref[d, pl.ds(rows, SIDE), :].astype(F32)
        mean, square = (
            side[i : i + panels] + side[i + panels : i + 2 * panels] + side[i + 2 * panels : i + 3 * panels]
            for i in (0, 3 * panels)
        )
        size = 2 * RIM * panels
        seams.append(side[6 * panels : 6 * panels + size] + side[6 * panels + size : 6 * panels + 2 * size])
        squares = squares + square
        scale = jnp.sqrt(square)
        for m in range(panels):
            mean_ref[d : d + 1, m * maps : (m + 1) * maps] = mean[m : m + 1]
            scale_ref[d : d + 1, m * maps : (m + 1) * maps] = scale[m : m + 1]
    for y in range(sum_y):
        seam = seams[(sum_x - 1) * sum_y + y] + seams[(y + 1) % sum_y]
        for m in range(panels):
            mean_ref[pl.ds(parts + 2 * RIM * y, 2 * RIM), m * maps : (m + 1) * maps] = seam[
                2 * RIM * m : 2 * RIM * (m + 1)
            ]
    means = mean_ref[...]
    row = lax.broadcasted_iota(jnp.int32, (means.shape[0], 1), 0)
    weight = jnp.where(row < parts, float(count), 1.0)
    weight = jnp.where(row < sum_y, float(count - 2 * RIM), weight)
    dev = means - jnp.sum(means * weight, axis=0, keepdims=True) * (1.0 / total_bins)
    own = jnp.concatenate([squares[m : m + 1] for m in range(panels)], axis=1)
    spread = (own + jnp.sum(dev * dev * weight, axis=0, keepdims=True)) * (1.0 / total_bins)
    scales = scale_ref[...]
    y = lax.axis_index("y")
    x = lax.axis_index("xh")
    rows_panel = y // 2 + jnp.where(y % 2 == lax.axis_index("core"), 0, halves)
    for m in range(panels):

        @pl.when(rows_panel == m)
        def _():
            cols = slice(m * maps, (m + 1) * maps)
            between_ref[...] = dot_tn(dev[:, cols] * weight, dev[:, : halves * maps])
            spread_ref[...] = jnp.transpose(jnp.broadcast_to(spread[:, cols], (maps, maps)))
            column = jnp.concatenate([scales[:, cols], jnp.zeros((maps - parts, maps), F32)], axis=0)
            column_ref[...] = jnp.transpose(column)

    for z in range(blocks):
        spot = pl.ds(pl.multiple_of((z * sum_x + x) * per, per), per)
        column = column_ref[spot, :]
        acc = [between_ref[spot, m * maps : (m + 1) * maps] for m in range(halves)]
        for d in range(parts):
            by_row = jnp.broadcast_to(column[:, d : d + 1], (per, maps))
            for m in range(halves):
                code = in_ref[d, pl.ds((m * blocks + z) * per, per), :].astype(F32)
                by_lane = scales[d : d + 1, m * maps : (m + 1) * maps]
                acc[m] = acc[m] + decode(code) * by_row * by_lane
        for m in range(halves):
            bottom = jnp.sqrt(spread_ref[spot, :] * spread[:, m * maps : (m + 1) * maps])
            for j in range(pairs):
                dest = place(m, z, j, blocks, pairs)
                part = slice(j * tile, (j + 1) * tile)
                out_ref[dest, pl.ds(0, tile), :] = acc[m][part] * (1.0 / total_bins)
                out_ref[dest, pl.ds(tile, tile), :] = bottom[part]


def summed(received, blocks, halves, pairs, sum_y, sum_x, count):
    parts = received.shape[0]
    tile = (received.shape[1] - SIDE) // (halves * blocks * pairs)
    total = 2 * halves * 128
    vmem = pl.BlockSpec(memory_space=pltpu.VMEM)
    return pl.pallas_call(
        lambda *refs: sum_kernel(blocks, halves, pairs, sum_y, sum_x, count, *refs),
        in_specs=[vmem],
        out_specs=vmem,
        out_shape=jax.ShapeDtypeStruct((halves * blocks * pairs, 2 * tile, 128), F32),
        scratch_shapes=[
            pltpu.VMEM((parts + 2 * RIM * sum_y, total), F32),
            pltpu.VMEM((parts, total), F32),
            pltpu.VMEM((128, total // 2), F32),
            pltpu.VMEM((128, 128), F32),
            pltpu.VMEM((128, 128), F32),
        ],
        compiler_params=params(),
        name="sum_parts",
    )(received)


def final_kernel(in_ref, gram_ref, scc_ref):
    strata, rows, _ = in_ref.shape
    per = rows // 2
    top = jnp.zeros((per, 128), F32)
    bottom = jnp.zeros((per, 128), F32)
    for k in range(strata):
        tile = in_ref[k, pl.ds(0, per), :]
        gram_ref[:, k, :] = tile
        top = top + tile
        bottom = bottom + in_ref[k, pl.ds(per, per), :]
    scc_ref[...] = top / bottom


def final(received):
    strata, rows, lanes = received.shape
    vmem = pl.BlockSpec(memory_space=pltpu.VMEM)
    return pl.pallas_call(
        final_kernel,
        in_specs=[vmem],
        out_specs=[vmem, vmem],
        out_shape=[
            jax.ShapeDtypeStruct((rows // 2, strata, lanes), F32),
            jax.ShapeDtypeStruct((rows // 2, lanes), F32),
        ],
        compiler_params=params(),
        name="final",
    )(received)


def body(band_maps, stratum_ids, half_width):
    maps, wide, bins = band_maps.shape
    blocks, halves, pairs, sum_y, sum_x = (lax.axis_size(a) for a in ("zl", "zh", "xl", "y", "xh"))
    edge, band_maps = edges(pltpu.with_memory_space_constraint(band_maps, pltpu.HBM))
    behind = lax.ppermute(edge, HALO_AXES, to_next())
    ready = inner(band_maps, stratum_ids, half_width)
    strata = smoothed(*ready, behind, stratum_ids, half_width)
    strata = lax.all_to_all(strata, STRATA_AXES, 0, 0, tiled=True)
    other = lax.ppermute(strata, "core", [(0, 1), (1, 0)])
    parts = partial_gram(strata, other, blocks, halves, pairs, sum_y, sum_x)
    parts = lax.all_to_all(parts, SUM_AXES, 0, 0, tiled=True)
    tiles = summed(parts, blocks, halves, pairs, sum_y, sum_x, blocks * pairs * bins)
    tiles = lax.all_to_all(tiles, STRATA_AXES, 0, 0, tiled=True)
    gram, scc = final(tiles)
    return gram, scc


def solution(mesh):
    split = Mesh(mesh.devices.reshape(4, 4, 2, 2, 2, 2), BINS_AXES + MAPS_AXES)
    in_specs = (P(MAPS_AXES, None, BINS_AXES), P(), P())
    out_specs = (P(BINS_AXES, None, MAPS_AXES), P(BINS_AXES, MAPS_AXES))
    return jax.shard_map(body, mesh=split, in_specs=in_specs, out_specs=out_specs, check_vma=False)
```

```python
import jax
import jax.numpy as jnp
from jax import lax
from jax.experimental import pallas as pl
from jax.experimental.pallas import tpu as pltpu
from jax.sharding import Mesh, PartitionSpec as P

HMAX = 2
X_AXES = ("xh", "xl")
BINS_AXES = ("y", "zl") + X_AXES
MAPS_AXES = ("zh", "core")
HALO_AXES = BINS_AXES + ("zh",)
STRATA_AXES = ("zh", "xl", "zl")
SUM_AXES = ("xh", "y")
F32 = jnp.float32
BF16 = jnp.bfloat16
HALO = 4
HEAD = 8
RIM = 2
SIDE = 64
SPAN = 200.0
VMEM_LIMIT = 28 * 1024 * 1024


def place(zh, zl, xl, blocks, pairs):
    return (zh * pairs + xl) * blocks + zl


def to_next():
    zl, x, zh = (lax.axis_size(a) for a in ("zl", X_AXES, "zh"))
    pairs = []
    for y in range(lax.axis_size("y")):
        flat = [((y * zl + p // x % zl) * x + p % x) * zh + p // (x * zl) for p in range(zh * zl * x)]
        pairs += [(flat[p], flat[(p + 1) % len(flat)]) for p in range(len(flat))]
    return pairs


def params():
    return pltpu.CompilerParams(vmem_limit_bytes=VMEM_LIMIT)


def edge_kernel(band_ref, edge_ref, copy_ref, sems):
    maps, wide, bins = band_ref.shape
    copies = [
        pltpu.make_async_copy(band_ref.at[:, :, lanes], copy_ref.at[:, :, lanes], sems.at[half])
        for half, lanes in enumerate((pl.ds(bins - 128, 128), pl.ds(0, bins - 128)))
    ]
    for copy in copies:
        copy.start()
    column = lax.broadcasted_iota(jnp.int32, (128, 128), 0)
    part = lax.rem(lax.broadcasted_iota(jnp.int32, (128, 128), 1), HALO)
    pick = (column == 128 - HALO + part).astype(BF16)
    offset = lax.broadcasted_iota(jnp.int32, (wide, 128), 0)
    lane = lax.broadcasted_iota(jnp.int32, (wide, 128), 1)
    own = (lax.div(lane, HALO) == offset)[None]
    copies[0].wait()
    data = copy_ref[:, :, pl.ds(bins - 128, 128)].reshape(maps * wide, 128)
    spread = jnp.dot(data, pick, preferred_element_type=F32).reshape(maps, wide, 128)
    edge_ref[...] = jnp.sum(jnp.where(own, spread, 0.0), axis=1).astype(BF16)
    copies[1].wait()


def edges(band_maps):
    maps, wide, bins = band_maps.shape
    vmem = pl.BlockSpec(memory_space=pltpu.VMEM)
    return pl.pallas_call(
        edge_kernel,
        in_specs=[pl.BlockSpec(memory_space=pltpu.HBM)],
        out_specs=[vmem, vmem],
        out_shape=[
            jax.ShapeDtypeStruct((maps, 128), BF16),
            jax.ShapeDtypeStruct(band_maps.shape, BF16),
        ],
        scratch_shapes=[pltpu.SemaphoreType.DMA((2,))],
        compiler_params=params(),
        cost_estimate=pl.CostEstimate(flops=2 * maps * wide * 128 * 128, bytes_accessed=2**22, transcendentals=0),
        name="edges",
    )(band_maps)


def windows(planes, win_ref, rows):
    wide = len(planes)
    for mid in range(1, wide - 1):
        one = planes[mid - 1] + planes[mid] + planes[mid + 1]
        win_ref[0, mid, rows, :] = one
        if 2 <= mid < wide - 2:
            win_ref[1, mid, rows, :] = one + (planes[mid - 2] + planes[mid + 2])


def box_of(win_ref, wider, centre):
    h = jnp.where(wider, 1, 0)
    reach = jnp.where(wider, 2, 0)
    outer = jnp.where(wider, 1.0, 0.0)
    scale = jnp.where(wider, 1.0 / 25.0, 1.0 / 9.0)

    def box(at, size):
        acc = win_ref[h, centre, pl.ds(at, size), :]
        acc = acc + win_ref[h, centre + 1, pl.ds(at - 1, size), :]
        acc = acc + win_ref[h, centre - 1, pl.ds(at + 1, size), :]
        far = win_ref[h, centre + reach, pl.ds(at - 2, size), :]
        far = far + win_ref[h, centre - reach, pl.ds(at + 2, size), :]
        return (acc + far * outer) * scale

    return box


def inner_kernel(
    ids_ref, half_ref, band_ref, sums_ref, total_ref, first_win_ref, last_win_ref, plane_ref, turned_ref, win_ref, perm_ref
):
    maps, wide, bins = band_ref.shape
    strata = sums_ref.shape[0]
    r = lax.broadcasted_iota(jnp.int32, (8 * wide, 8 * wide), 0)
    c = lax.broadcasted_iota(jnp.int32, (8 * wide, 8 * wide), 1)
    perm_ref[...] = (c == lax.rem(r, 8) * wide + lax.div(r, 8)).astype(BF16)
    for g in range(0, maps, 16):
        pair = [
            jnp.dot(
                perm_ref[...], band_ref[pl.ds(g + 8 * j, 8)].reshape(8 * wide, bins), preferred_element_type=F32
            ).reshape(wide, 8, bins)
            for j in range(2)
        ]
        plane_ref[:, pl.ds(g, 16), :] = jnp.concatenate(pair, axis=1).astype(BF16)

    for d in range(wide):
        for half in range(bins // 128):
            tile = plane_ref[d, :, half * 128 : half * 128 + 128]
            turned_ref[d, pl.ds(half * 128, 128), :] = jnp.transpose(tile).astype(F32)

    def some(i, carry):
        rows = pl.ds(pl.multiple_of(i * 16, 16), 16)
        windows([turned_ref[d, rows, :] for d in range(wide)], win_ref, rows)
        return carry

    lax.fori_loop(0, bins // 16, some, 0)
    first_win_ref[...] = win_ref[:, :, pl.ds(0, 8), :]
    last_win_ref[...] = win_ref[:, :, pl.ds(bins - 8, 8), :]

    def stratum(k, carry):
        box = box_of(win_ref, half_ref[k] >= 2, ids_ref[k])
        total = jnp.zeros((1, maps), F32)
        for at in range(0, bins - HEAD, 64):
            size = min(64, bins - HEAD - at)
            part = box(at + HEAD - RIM, size)
            sums_ref[k, pl.ds(at, size), :] = part
            total = total + jnp.sum(part, axis=0, keepdims=True)
        total_ref[k] = jnp.broadcast_to(total, (8, maps))
        return carry

    lax.fori_loop(0, strata, stratum, 0, unroll=4)


def inner(band_maps, stratum_ids, half_width):
    maps, wide, bins = band_maps.shape
    strata = stratum_ids.shape[0]
    smem = pl.BlockSpec(memory_space=pltpu.SMEM)
    vmem = pl.BlockSpec(memory_space=pltpu.VMEM)
    return pl.pallas_call(
        inner_kernel,
        in_specs=[smem, smem, vmem],
        out_specs=[vmem, vmem, vmem, vmem],
        out_shape=[
            jax.ShapeDtypeStruct((strata, bins - HEAD, maps), F32),
            jax.ShapeDtypeStruct((strata, 8, maps), F32),
            jax.ShapeDtypeStruct((2, wide, 8, maps), F32),
            jax.ShapeDtypeStruct((2, wide, 8, maps), F32),
        ],
        scratch_shapes=[
            pltpu.VMEM((wide, maps, bins), BF16),
            pltpu.VMEM((wide, bins, maps), F32),
            pltpu.VMEM((2, wide, bins, maps), F32),
            pltpu.VMEM((8 * wide, 8 * wide), BF16),
        ],
        compiler_params=params(),
        cost_estimate=pl.CostEstimate(flops=2 * maps * wide * bins * 256, bytes_accessed=2**22, transcendentals=0),
        name="inner",
    )(stratum_ids, half_width, band_maps)


def words_of(value):
    hi = value.astype(BF16).astype(F32)
    mid = (value - hi).astype(BF16).astype(F32)
    return hi, mid, value - hi - mid


def smooth_kernel(
    ids_ref, half_ref, sums_ref, total_ref, first_win_ref, last_win_ref, behind_ref, out_ref, start_ref, stop_ref
):
    strata, ready, maps = sums_ref.shape
    wide = first_win_ref.shape[1]
    bins = ready + HEAD
    y, z, x = (lax.axis_index(a) for a in ("y", "zl", X_AXES))
    last_y, last_z, last_x = (lax.axis_size(a) - 1 for a in ("y", "zl", X_AXES))
    before = (z == last_z) & (x == last_x)
    after = (z == 0) & (x == 0)
    behind = jnp.where(after, 0.0, jnp.transpose(behind_ref[...].astype(F32)))
    row8 = lax.broadcasted_iota(jnp.int32, (8, maps), 0)
    heads = []
    for d in range(wide):
        at = HALO * d
        tile = pltpu.roll(behind[at // 8 * 8 : at // 8 * 8 + 8], (8 - HALO - at % 8) % 8, axis=0)
        heads.append(jnp.where(row8 >= 8 - HALO, tile, 0.0))
    windows(heads, start_ref, pl.ds(0, 8))
    start_ref[:, :, pl.ds(8, 8), :] = first_win_ref[...]
    stop_ref[:, :, pl.ds(0, 8), :] = last_win_ref[...]
    stop_ref[:, :, pl.ds(8, 8), :] = jnp.zeros((2, wide, 8, maps), F32)

    row = lax.broadcasted_iota(jnp.int32, (16, maps), 0)
    empty = after & (row8 < 2 * RIM)
    seam_before = before & (row8 < 2 * RIM) & ((y < last_y) | (row8 < RIM))
    seam_after = after & (row8 < 2 * RIM) & ((y > 0) | (row8 >= RIM))
    per_slot = jnp.where(after, 1.0 / (bins - 2 * RIM), 1.0 / bins)

    def stratum(k, carry):
        wider, centre = half_ref[k] >= 2, ids_ref[k]
        head = box_of(start_ref, wider, centre)(8 - RIM, 8)
        total = total_ref[k][:1] + jnp.sum(jnp.where(empty, 0.0, head), axis=0, keepdims=True)
        mean = total * per_slot
        square = jnp.zeros((1, maps), F32)
        for at in range(0, bins, 64):
            if at == 0:
                part = [jnp.where(empty, mean, head), sums_ref[k, pl.ds(0, 64 - HEAD), :]]
                part = jnp.concatenate(part, axis=0)
            else:
                part = sums_ref[k, pl.ds(at - HEAD, 64), :]
            part = part - mean
            square = square + jnp.sum(part * part, axis=0, keepdims=True)
            out_ref[k, pl.ds(at, 64), :] = part.astype(BF16)
        seam = jnp.where(seam_before, box_of(stop_ref, wider, centre)(8 - RIM, 8), 0.0)
        seam = seam + jnp.where(seam_after, head, 0.0)
        side = jnp.zeros((16, maps), F32)
        for i, value in enumerate(words_of(mean) + words_of(square)):
            side = jnp.where(row == i, value, side)
        for i, value in enumerate(words_of(seam)[:2]):
            value = jnp.concatenate([value, jnp.zeros((8, maps), F32)], axis=0)
            side = side + pltpu.roll(value, 6 + 2 * RIM * i, axis=0)
        out_ref[k, pl.ds(bins, 16), :] = side.astype(BF16)
        return carry

    lax.fori_loop(0, strata, stratum, 0, unroll=4)


def smoothed(sums, total, first_win, last_win, behind, stratum_ids, half_width):
    strata, ready, maps = sums.shape
    wide = first_win.shape[1]
    smem = pl.BlockSpec(memory_space=pltpu.SMEM)
    vmem = pl.BlockSpec(memory_space=pltpu.VMEM)
    return pl.pallas_call(
        smooth_kernel,
        in_specs=[smem, smem] + [vmem] * 5,
        out_specs=vmem,
        out_shape=jax.ShapeDtypeStruct((strata, ready + HEAD + 16, maps), BF16),
        scratch_shapes=[
            pltpu.VMEM((2, wide, 16, maps), F32),
            pltpu.VMEM((2, wide, 16, maps), F32),
        ],
        compiler_params=params(),
        name="smooth",
    )(stratum_ids, half_width, sums, total, first_win, last_win, behind)


def encode(r):
    size = jnp.exp2(jnp.abs(r) * SPAN - 0.5 * SPAN)
    return jnp.where(r < 0.0, -size, size)


def decode(code):
    size = jnp.log2(jnp.abs(code)) * (1.0 / SPAN) + 0.5
    return jnp.where(code < 0.0, -size, size)


def dot_tn(a, b):
    return lax.dot_general(
        a, b, (((0,), (0,)), ((), ())), precision=lax.Precision.HIGHEST, preferred_element_type=F32
    )


def gram_kernel(blocks, halves, pairs, sum_y, sum_x, bins, own_ref, other_ref, out_ref, data_ref, mean_ref, gram_ref):
    maps = 128
    panels = 2 * halves
    total = panels * maps
    mine = halves * maps
    count_blocks = blocks * pairs
    squares, seams = [], []
    for m in range(panels):
        in_ref = (own_ref, other_ref)[m // halves]
        square, seam = [], []
        for z in range(blocks):
            for x in range(pairs):
                src = place(m % halves, z, x, blocks, pairs)
                b = z * pairs + x
                data_ref[pl.ds(b * bins, bins), pl.ds(m * maps, maps)] = in_ref[src, pl.ds(0, bins), :]
                words = in_ref[src, pl.ds(bins, 16), :].astype(F32)
                mean_ref[b : b + 1, m * maps : (m + 1) * maps] = words[0:1] + words[1:2] + words[2:3]
                square.append(words[3:4] + words[4:5] + words[5:6])
                seam.append(words[6:10] + words[10:14])
        squares.append(sum(square))
        seams.append(sum(seam))
    means = mean_ref[...]
    short = lax.axis_index("xh") == 0
    b = lax.broadcasted_iota(jnp.int32, (count_blocks, 1), 0)
    count = jnp.where(short & (b == 0), float(bins - 2 * RIM), float(bins))
    centre = jnp.sum(means * count, axis=0, keepdims=True)
    centre = centre * jnp.where(short, 1.0 / (count_blocks * bins - 2 * RIM), 1.0 / (count_blocks * bins))
    dev = means - centre
    hi, mid, low = words_of(dev[:, :mine])
    left_hi, left_mid, left_low = words_of(dev * count)
    pad = -6 * count_blocks % 32
    left = [left_hi, left_hi, left_mid, left_mid, left_hi, left_low, jnp.zeros((pad, total), F32)]
    right = [hi, mid, hi, mid, low, hi, jnp.zeros((pad, mine), F32)]
    left, right = (jnp.concatenate(a, axis=0).astype(BF16) for a in (left, right))
    tn = (((0,), (0,)), ((), ()))
    gram_ref[...] = lax.dot_general(
        data_ref[...], data_ref[:, :mine], tn, preferred_element_type=F32
    ) + lax.dot_general(left, right, tn, preferred_element_type=F32)
    squares = jnp.concatenate(squares, axis=1) + jnp.sum(dev * dev * count, axis=0, keepdims=True)
    by_lane = jnp.where(squares > 0.0, lax.rsqrt(squares), 0.0)

    def rows_of(line):
        return jnp.concatenate([line[:, m * maps : (m + 1) * maps] for m in range(panels)], axis=0)

    side = words_of(rows_of(centre)) + words_of(rows_of(squares)) + words_of(jnp.concatenate(seams, axis=0))[:2]
    side += (jnp.zeros((SIDE - (6 + 4 * RIM) * panels, maps), F32),)
    side = jnp.concatenate(side, axis=0).astype(BF16)
    core = lax.axis_index("core")
    per = maps // (blocks * sum_x)
    for q in range(panels):
        y = (q % halves) * 2 + (core if q < halves else 1 - core)
        by_row = jnp.transpose(jnp.broadcast_to(by_lane[:, q * maps : (q + 1) * maps], (maps, maps)))
        for m in range(halves):
            cols = slice(m * maps, (m + 1) * maps)
            code = encode(gram_ref[pl.ds(q * maps, maps), cols] * by_row * by_lane[:, cols]).astype(BF16)
            for x in range(sum_x):
                for z in range(blocks):
                    at = (z * sum_x + x) * per
                    out_ref[x * sum_y + y, pl.ds((m * blocks + z) * per, per), :] = code[at : at + per]
    for d in range(sum_x * sum_y):
        out_ref[d, pl.ds(halves * blocks * per, SIDE), :] = side


def partial_gram(own, other, blocks, halves, pairs, sum_y, sum_x):
    bins = own.shape[1] - 16
    total = 2 * halves * 128
    per = 128 // (blocks * sum_x)
    vmem = pl.BlockSpec(memory_space=pltpu.VMEM)
    return pl.pallas_call(
        lambda *refs: gram_kernel(blocks, halves, pairs, sum_y, sum_x, bins, *refs),
        in_specs=[vmem, vmem],
        out_specs=vmem,
        out_shape=jax.ShapeDtypeStruct((sum_y * sum_x, halves * blocks * per + SIDE, 128), BF16),
        scratch_shapes=[
            pltpu.VMEM((blocks * pairs * bins, total), BF16),
            pltpu.VMEM((blocks * pairs, total), F32),
            pltpu.VMEM((total, total // 2), F32),
        ],
        compiler_params=params(),
        name="partial_gram",
    )(own, other)


def sum_kernel(
    blocks, halves, pairs, sum_y, sum_x, count, in_ref, out_ref, mean_ref, scale_ref, between_ref, spread_ref, column_ref
):
    maps = 128
    panels = 2 * halves
    parts = in_ref.shape[0]
    rows = in_ref.shape[1] - SIDE
    per = rows // (halves * blocks)
    tile = per // pairs
    total_bins = float(count * parts)
    squares = jnp.zeros((panels, maps), F32)
    seams = []
    for d in range(parts):
        side = in_ref[d, pl.ds(rows, SIDE), :].astype(F32)
        mean, square = (
            side[i : i + panels] + side[i + panels : i + 2 * panels] + side[i + 2 * panels : i + 3 * panels]
            for i in (0, 3 * panels)
        )
        size = 2 * RIM * panels
        seams.append(side[6 * panels : 6 * panels + size] + side[6 * panels + size : 6 * panels + 2 * size])
        squares = squares + square
        scale = jnp.sqrt(square)
        for m in range(panels):
            mean_ref[d : d + 1, m * maps : (m + 1) * maps] = mean[m : m + 1]
            scale_ref[d : d + 1, m * maps : (m + 1) * maps] = scale[m : m + 1]
    for y in range(sum_y):
        seam = seams[(sum_x - 1) * sum_y + y] + seams[(y + 1) % sum_y]
        for m in range(panels):
            mean_ref[pl.ds(parts + 2 * RIM * y, 2 * RIM), m * maps : (m + 1) * maps] = seam[
                2 * RIM * m : 2 * RIM * (m + 1)
            ]
    means = mean_ref[...]
    row = lax.broadcasted_iota(jnp.int32, (means.shape[0], 1), 0)
    weight = jnp.where(row < parts, float(count), 1.0)
    weight = jnp.where(row < sum_y, float(count - 2 * RIM), weight)
    dev = means - jnp.sum(means * weight, axis=0, keepdims=True) * (1.0 / total_bins)
    own = jnp.concatenate([squares[m : m + 1] for m in range(panels)], axis=1)
    spread = (own + jnp.sum(dev * dev * weight, axis=0, keepdims=True)) * (1.0 / total_bins)
    scales = scale_ref[...]
    y = lax.axis_index("y")
    x = lax.axis_index("xh")
    rows_panel = y // 2 + jnp.where(y % 2 == lax.axis_index("core"), 0, halves)
    for m in range(panels):

        @pl.when(rows_panel == m)
        def _():
            cols = slice(m * maps, (m + 1) * maps)
            between_ref[...] = dot_tn(dev[:, cols] * weight, dev[:, : halves * maps])
            spread_ref[...] = jnp.transpose(jnp.broadcast_to(spread[:, cols], (maps, maps)))
            column = jnp.concatenate([scales[:, cols], jnp.zeros((maps - parts, maps), F32)], axis=0)
            column_ref[...] = jnp.transpose(column)

    for z in range(blocks):
        spot = pl.ds(pl.multiple_of((z * sum_x + x) * per, per), per)
        column = column_ref[spot, :]
        acc = [between_ref[spot, m * maps : (m + 1) * maps] for m in range(halves)]
        for d in range(parts):
            by_row = jnp.broadcast_to(column[:, d : d + 1], (per, maps))
            for m in range(halves):
                code = in_ref[d, pl.ds((m * blocks + z) * per, per), :].astype(F32)
                by_lane = scales[d : d + 1, m * maps : (m + 1) * maps]
                acc[m] = acc[m] + decode(code) * by_row * by_lane
        for m in range(halves):
            bottom = jnp.sqrt(spread_ref[spot, :] * spread[:, m * maps : (m + 1) * maps])
            for j in range(pairs):
                dest = place(m, z, j, blocks, pairs)
                part = slice(j * tile, (j + 1) * tile)
                out_ref[dest, pl.ds(0, tile), :] = acc[m][part] * (1.0 / total_bins)
                out_ref[dest, pl.ds(tile, tile), :] = bottom[part]


def summed(received, blocks, halves, pairs, sum_y, sum_x, count):
    parts = received.shape[0]
    tile = (received.shape[1] - SIDE) // (halves * blocks * pairs)
    total = 2 * halves * 128
    vmem = pl.BlockSpec(memory_space=pltpu.VMEM)
    return pl.pallas_call(
        lambda *refs: sum_kernel(blocks, halves, pairs, sum_y, sum_x, count, *refs),
        in_specs=[vmem],
        out_specs=vmem,
        out_shape=jax.ShapeDtypeStruct((halves * blocks * pairs, 2 * tile, 128), F32),
        scratch_shapes=[
            pltpu.VMEM((parts + 2 * RIM * sum_y, total), F32),
            pltpu.VMEM((parts, total), F32),
            pltpu.VMEM((128, total // 2), F32),
            pltpu.VMEM((128, 128), F32),
            pltpu.VMEM((128, 128), F32),
        ],
        compiler_params=params(),
        name="sum_parts",
    )(received)


def final_kernel(in_ref, gram_ref, scc_ref):
    strata, rows, _ = in_ref.shape
    per = rows // 2
    top = jnp.zeros((per, 128), F32)
    bottom = jnp.zeros((per, 128), F32)
    for k in range(strata):
        tile = in_ref[k, pl.ds(0, per), :]
        gram_ref[:, k, :] = tile
        top = top + tile
        bottom = bottom + in_ref[k, pl.ds(per, per), :]
    scc_ref[...] = top / bottom


def final(received):
    strata, rows, lanes = received.shape
    vmem = pl.BlockSpec(memory_space=pltpu.VMEM)
    return pl.pallas_call(
        final_kernel,
        in_specs=[vmem],
        out_specs=[vmem, vmem],
        out_shape=[
            jax.ShapeDtypeStruct((rows // 2, strata, lanes), F32),
            jax.ShapeDtypeStruct((rows // 2, lanes), F32),
        ],
        compiler_params=params(),
        name="final",
    )(received)


def body(band_maps, stratum_ids, half_width):
    maps, wide, bins = band_maps.shape
    blocks, halves, pairs, sum_y, sum_x = (lax.axis_size(a) for a in ("zl", "zh", "xl", "y", "xh"))
    edge, band_maps = edges(pltpu.with_memory_space_constraint(band_maps, pltpu.HBM))
    behind = lax.ppermute(edge, HALO_AXES, to_next())
    ready = inner(band_maps, stratum_ids, half_width)
    strata = smoothed(*ready, behind, stratum_ids, half_width)
    strata = lax.all_to_all(strata, STRATA_AXES, 0, 0, tiled=True)
    other = lax.ppermute(strata, "core", [(0, 1), (1, 0)])
    parts = partial_gram(strata, other, blocks, halves, pairs, sum_y, sum_x)
    parts = lax.all_to_all(parts, SUM_AXES, 0, 0, tiled=True)
    tiles = summed(parts, blocks, halves, pairs, sum_y, sum_x, blocks * pairs * bins)
    tiles = lax.all_to_all(tiles, STRATA_AXES, 0, 0, tiled=True)
    gram, scc = final(tiles)
    return gram, scc


def solution(mesh):
    split = Mesh(mesh.devices.reshape(4, 4, 2, 2, 2, 2), BINS_AXES + MAPS_AXES)
    in_specs = (P(MAPS_AXES, None, BINS_AXES), P(), P())
    out_specs = (P(BINS_AXES, None, MAPS_AXES), P(BINS_AXES, MAPS_AXES))
    return jax.shard_map(body, mesh=split, in_specs=in_specs, out_specs=out_specs, check_vma=False)
```

```python
import jax
import jax.numpy as jnp
from jax import lax
from jax.experimental import pallas as pl
from jax.experimental.pallas import tpu as pltpu
from jax.sharding import Mesh, PartitionSpec as P

HMAX = 2
X_AXES = ("xh", "xl")
BINS_AXES = ("y", "zl") + X_AXES
MAPS_AXES = ("zh", "core")
HALO_AXES = BINS_AXES + ("zh",)
STRATA_AXES = ("zh", "xl", "zl")
SUM_AXES = ("xh", "y")
F32 = jnp.float32
BF16 = jnp.bfloat16
HALO = 4
HEAD = 8
RIM = 2
SIDE = 64
SPAN = 200.0
VMEM_LIMIT = 28 * 1024 * 1024


def place(zh, zl, xl, blocks, pairs):
    return (zh * pairs + xl) * blocks + zl


def to_next():
    zl, x, zh = (lax.axis_size(a) for a in ("zl", X_AXES, "zh"))
    pairs = []
    for y in range(lax.axis_size("y")):
        flat = [((y * zl + p // x % zl) * x + p % x) * zh + p // (x * zl) for p in range(zh * zl * x)]
        pairs += [(flat[p], flat[(p + 1) % len(flat)]) for p in range(len(flat))]
    return pairs


def params():
    return pltpu.CompilerParams(vmem_limit_bytes=VMEM_LIMIT)


def edge_kernel(band_ref, edge_ref, copy_ref, sems):
    maps, wide, bins = band_ref.shape
    copies = [
        pltpu.make_async_copy(band_ref.at[:, :, lanes], copy_ref.at[:, :, lanes], sems.at[half])
        for half, lanes in enumerate((pl.ds(bins - 128, 128), pl.ds(0, bins - 128)))
    ]
    for copy in copies:
        copy.start()
    column = lax.broadcasted_iota(jnp.int32, (128, 128), 0)
    part = lax.rem(lax.broadcasted_iota(jnp.int32, (128, 128), 1), HALO)
    pick = (column == 128 - HALO + part).astype(BF16)
    offset = lax.broadcasted_iota(jnp.int32, (wide, 128), 0)
    lane = lax.broadcasted_iota(jnp.int32, (wide, 128), 1)
    own = (lax.div(lane, HALO) == offset)[None]
    copies[0].wait()
    data = copy_ref[:, :, pl.ds(bins - 128, 128)].reshape(maps * wide, 128)
    spread = jnp.dot(data, pick, preferred_element_type=F32).reshape(maps, wide, 128)
    edge_ref[...] = jnp.sum(jnp.where(own, spread, 0.0), axis=1).astype(BF16)
    copies[1].wait()


def edges(band_maps):
    maps, wide, bins = band_maps.shape
    vmem = pl.BlockSpec(memory_space=pltpu.VMEM)
    return pl.pallas_call(
        edge_kernel,
        in_specs=[pl.BlockSpec(memory_space=pltpu.HBM)],
        out_specs=[vmem, vmem],
        out_shape=[
            jax.ShapeDtypeStruct((maps, 128), BF16),
            jax.ShapeDtypeStruct(band_maps.shape, BF16),
        ],
        scratch_shapes=[pltpu.SemaphoreType.DMA((2,))],
        compiler_params=params(),
        cost_estimate=pl.CostEstimate(flops=2 * maps * wide * 128 * 128, bytes_accessed=2**22, transcendentals=0),
        name="edges",
    )(band_maps)


def windows(planes, win_ref, rows):
    wide = len(planes)
    for mid in range(1, wide - 1):
        one = planes[mid - 1] + planes[mid] + planes[mid + 1]
        win_ref[0, mid, rows, :] = one
        if 2 <= mid < wide - 2:
            win_ref[1, mid, rows, :] = one + (planes[mid - 2] + planes[mid + 2])


def box_of(win_ref, wider, centre):
    h = jnp.where(wider, 1, 0)
    reach = jnp.where(wider, 2, 0)
    outer = jnp.where(wider, 1.0, 0.0)
    scale = jnp.where(wider, 1.0 / 25.0, 1.0 / 9.0)

    def box(at, size):
        acc = win_ref[h, centre, pl.ds(at, size), :]
        acc = acc + win_ref[h, centre + 1, pl.ds(at - 1, size), :]
        acc = acc + win_ref[h, centre - 1, pl.ds(at + 1, size), :]
        far = win_ref[h, centre + reach, pl.ds(at - 2, size), :]
        far = far + win_ref[h, centre - reach, pl.ds(at + 2, size), :]
        return (acc + far * outer) * scale

    return box


def inner_kernel(
    ids_ref, half_ref, band_ref, sums_ref, total_ref, first_win_ref, last_win_ref, plane_ref, turned_ref, win_ref, perm_ref
):
    maps, wide, bins = band_ref.shape
    strata = sums_ref.shape[0]
    r = lax.broadcasted_iota(jnp.int32, (8 * wide, 8 * wide), 0)
    c = lax.broadcasted_iota(jnp.int32, (8 * wide, 8 * wide), 1)
    perm_ref[...] = (c == lax.rem(r, 8) * wide + lax.div(r, 8)).astype(BF16)
    for g in range(0, maps, 16):
        pair = [
            jnp.dot(
                perm_ref[...], band_ref[pl.ds(g + 8 * j, 8)].reshape(8 * wide, bins), preferred_element_type=F32
            ).reshape(wide, 8, bins)
            for j in range(2)
        ]
        plane_ref[:, pl.ds(g, 16), :] = jnp.concatenate(pair, axis=1).astype(BF16)

    for d in range(wide):
        for half in range(bins // 128):
            tile = plane_ref[d, :, half * 128 : half * 128 + 128]
            turned_ref[d, pl.ds(half * 128, 128), :] = jnp.transpose(tile).astype(F32)

    def some(i, carry):
        rows = pl.ds(pl.multiple_of(i * 16, 16), 16)
        windows([turned_ref[d, rows, :] for d in range(wide)], win_ref, rows)
        return carry

    lax.fori_loop(0, bins // 16, some, 0)
    first_win_ref[...] = win_ref[:, :, pl.ds(0, 8), :]
    last_win_ref[...] = win_ref[:, :, pl.ds(bins - 8, 8), :]

    def stratum(k, carry):
        box = box_of(win_ref, half_ref[k] >= 2, ids_ref[k])
        total = jnp.zeros((1, maps), F32)
        for at in range(0, bins - HEAD, 64):
            size = min(64, bins - HEAD - at)
            part = box(at + HEAD - RIM, size)
            sums_ref[k, pl.ds(at, size), :] = part
            total = total + jnp.sum(part, axis=0, keepdims=True)
        total_ref[k] = jnp.broadcast_to(total, (8, maps))
        return carry

    lax.fori_loop(0, strata, stratum, 0, unroll=4)


def inner(band_maps, stratum_ids, half_width):
    maps, wide, bins = band_maps.shape
    strata = stratum_ids.shape[0]
    smem = pl.BlockSpec(memory_space=pltpu.SMEM)
    vmem = pl.BlockSpec(memory_space=pltpu.VMEM)
    return pl.pallas_call(
        inner_kernel,
        in_specs=[smem, smem, vmem],
        out_specs=[vmem, vmem, vmem, vmem],
        out_shape=[
            jax.ShapeDtypeStruct((strata, bins - HEAD, maps), F32),
            jax.ShapeDtypeStruct((strata, 8, maps), F32),
            jax.ShapeDtypeStruct((2, wide, 8, maps), F32),
            jax.ShapeDtypeStruct((2, wide, 8, maps), F32),
        ],
        scratch_shapes=[
            pltpu.VMEM((wide, maps, bins), BF16),
            pltpu.VMEM((wide, bins, maps), F32),
            pltpu.VMEM((2, wide, bins, maps), F32),
            pltpu.VMEM((8 * wide, 8 * wide), BF16),
        ],
        compiler_params=params(),
        cost_estimate=pl.CostEstimate(flops=2 * maps * wide * bins * 256, bytes_accessed=2**22, transcendentals=0),
        name="inner",
    )(stratum_ids, half_width, band_maps)


def words_of(value):
    hi = value.astype(BF16).astype(F32)
    mid = (value - hi).astype(BF16).astype(F32)
    return hi, mid, value - hi - mid


def smooth_kernel(
    ids_ref, half_ref, sums_ref, total_ref, first_win_ref, last_win_ref, behind_ref, out_ref, start_ref, stop_ref
):
    strata, ready, maps = sums_ref.shape
    wide = first_win_ref.shape[1]
    bins = ready + HEAD
    y, z, x = (lax.axis_index(a) for a in ("y", "zl", X_AXES))
    last_y, last_z, last_x = (lax.axis_size(a) - 1 for a in ("y", "zl", X_AXES))
    before = (z == last_z) & (x == last_x)
    after = (z == 0) & (x == 0)
    behind = jnp.where(after, 0.0, jnp.transpose(behind_ref[...].astype(F32)))
    row8 = lax.broadcasted_iota(jnp.int32, (8, maps), 0)
    heads = []
    for d in range(wide):
        at = HALO * d
        tile = pltpu.roll(behind[at // 8 * 8 : at // 8 * 8 + 8], (8 - HALO - at % 8) % 8, axis=0)
        heads.append(jnp.where(row8 >= 8 - HALO, tile, 0.0))
    windows(heads, start_ref, pl.ds(0, 8))
    start_ref[:, :, pl.ds(8, 8), :] = first_win_ref[...]
    stop_ref[:, :, pl.ds(0, 8), :] = last_win_ref[...]
    stop_ref[:, :, pl.ds(8, 8), :] = jnp.zeros((2, wide, 8, maps), F32)

    row = lax.broadcasted_iota(jnp.int32, (16, maps), 0)
    empty = after & (row8 < 2 * RIM)
    seam_before = before & (row8 < 2 * RIM) & ((y < last_y) | (row8 < RIM))
    seam_after = after & (row8 < 2 * RIM) & ((y > 0) | (row8 >= RIM))
    per_slot = jnp.where(after, 1.0 / (bins - 2 * RIM), 1.0 / bins)

    def stratum(k, carry):
        wider, centre = half_ref[k] >= 2, ids_ref[k]
        head = box_of(start_ref, wider, centre)(8 - RIM, 8)
        total = total_ref[k][:1] + jnp.sum(jnp.where(empty, 0.0, head), axis=0, keepdims=True)
        mean = total * per_slot
        square = jnp.zeros((1, maps), F32)
        for at in range(0, bins, 64):
            if at == 0:
                part = [jnp.where(empty, mean, head), sums_ref[k, pl.ds(0, 64 - HEAD), :]]
                part = jnp.concatenate(part, axis=0)
            else:
                part = sums_ref[k, pl.ds(at - HEAD, 64), :]
            part = part - mean
            square = square + jnp.sum(part * part, axis=0, keepdims=True)
            out_ref[k, pl.ds(at, 64), :] = part.astype(BF16)
        seam = jnp.where(seam_before, box_of(stop_ref, wider, centre)(8 - RIM, 8), 0.0)
        seam = seam + jnp.where(seam_after, head, 0.0)
        side = jnp.zeros((16, maps), F32)
        for i, value in enumerate(words_of(mean) + words_of(square)):
            side = jnp.where(row == i, value, side)
        for i, value in enumerate(words_of(seam)[:2]):
            value = jnp.concatenate([value, jnp.zeros((8, maps), F32)], axis=0)
            side = side + pltpu.roll(value, 6 + 2 * RIM * i, axis=0)
        out_ref[k, pl.ds(bins, 16), :] = side.astype(BF16)
        return carry

    lax.fori_loop(0, strata, stratum, 0, unroll=4)


def smoothed(sums, total, first_win, last_win, behind, stratum_ids, half_width):
    strata, ready, maps = sums.shape
    wide = first_win.shape[1]
    smem = pl.BlockSpec(memory_space=pltpu.SMEM)
    vmem = pl.BlockSpec(memory_space=pltpu.VMEM)
    return pl.pallas_call(
        smooth_kernel,
        in_specs=[smem, smem] + [vmem] * 5,
        out_specs=vmem,
        out_shape=jax.ShapeDtypeStruct((strata, ready + HEAD + 16, maps), BF16),
        scratch_shapes=[
            pltpu.VMEM((2, wide, 16, maps), F32),
            pltpu.VMEM((2, wide, 16, maps), F32),
        ],
        compiler_params=params(),
        name="smooth",
    )(stratum_ids, half_width, sums, total, first_win, last_win, behind)


def encode(r):
    size = jnp.exp2(jnp.abs(r) * SPAN - 0.5 * SPAN)
    return jnp.where(r < 0.0, -size, size)


def decode(code):
    size = jnp.log2(jnp.abs(code)) * (1.0 / SPAN) + 0.5
    return jnp.where(code < 0.0, -size, size)


def dot_tn(a, b):
    return lax.dot_general(
        a, b, (((0,), (0,)), ((), ())), precision=lax.Precision.HIGHEST, preferred_element_type=F32
    )


TN = (((0,), (0,)), ((), ()))


def gather_panels(in_ref, data_ref, blocks, halves, pairs, bins):
    for m in range(halves):
        for z in range(blocks):
            for x in range(pairs):
                src = place(m, z, x, blocks, pairs)
                rows = pl.ds((z * pairs + x) * bins, bins)
                data_ref[rows, pl.ds(m * 128, 128)] = in_ref[src, pl.ds(0, bins), :]


def own_kernel(blocks, halves, pairs, bins, own_ref, data_ref, gram_ref):
    gather_panels(own_ref, data_ref, blocks, halves, pairs, bins)
    data = data_ref[...]
    gram_ref[...] = lax.dot_general(data, data, TN, preferred_element_type=F32)


def own_gram(own, blocks, halves, pairs):
    bins = own.shape[1] - 16
    rows, mine = blocks * pairs * bins, halves * 128
    vmem = pl.BlockSpec(memory_space=pltpu.VMEM)
    return pl.pallas_call(
        lambda *refs: own_kernel(blocks, halves, pairs, bins, *refs),
        in_specs=[vmem],
        out_specs=[vmem, vmem],
        out_shape=[jax.ShapeDtypeStruct((rows, mine), BF16), jax.ShapeDtypeStruct((mine, mine), F32)],
        compiler_params=params(),
        cost_estimate=pl.CostEstimate(flops=2 * rows * mine * mine, bytes_accessed=2**21, transcendentals=0),
        name="own_gram",
    )(own)


def gram_kernel(
    blocks, halves, pairs, sum_y, sum_x, bins, own_ref, other_ref, mine_ref, square_ref, out_ref, data_ref, mean_ref, gram_ref
):
    maps = 128
    panels = 2 * halves
    total = panels * maps
    mine = halves * maps
    count_blocks = blocks * pairs
    gather_panels(other_ref, data_ref, blocks, halves, pairs, bins)
    squares, seams = [], []
    for m in range(panels):
        in_ref = (own_ref, other_ref)[m // halves]
        square, seam = [], []
        for z in range(blocks):
            for x in range(pairs):
                src = place(m % halves, z, x, blocks, pairs)
                b = z * pairs + x
                words = in_ref[src, pl.ds(bins, 16), :].astype(F32)
                mean_ref[b : b + 1, m * maps : (m + 1) * maps] = words[0:1] + words[1:2] + words[2:3]
                square.append(words[3:4] + words[4:5] + words[5:6])
                seam.append(words[6:10] + words[10:14])
        squares.append(sum(square))
        seams.append(sum(seam))
    means = mean_ref[...]
    short = lax.axis_index("xh") == 0
    b = lax.broadcasted_iota(jnp.int32, (count_blocks, 1), 0)
    count = jnp.where(short & (b == 0), float(bins - 2 * RIM), float(bins))
    centre = jnp.sum(means * count, axis=0, keepdims=True)
    centre = centre * jnp.where(short, 1.0 / (count_blocks * bins - 2 * RIM), 1.0 / (count_blocks * bins))
    dev = means - centre
    hi, mid, low = words_of(dev[:, :mine])
    left_hi, left_mid, left_low = words_of(dev * count)
    pad = -6 * count_blocks % 32
    left = [left_hi, left_hi, left_mid, left_mid, left_hi, left_low, jnp.zeros((pad, total), F32)]
    right = [hi, mid, hi, mid, low, hi, jnp.zeros((pad, mine), F32)]
    left, right = (jnp.concatenate(a, axis=0).astype(BF16) for a in (left, right))
    between = lax.dot_general(left, right, TN, preferred_element_type=F32)
    gram_ref[:mine] = square_ref[...] + between[:mine]
    gram_ref[mine:] = between[mine:] + lax.dot_general(
        data_ref[...], mine_ref[...], TN, preferred_element_type=F32
    )
    squares = jnp.concatenate(squares, axis=1) + jnp.sum(dev * dev * count, axis=0, keepdims=True)
    by_lane = jnp.where(squares > 0.0, lax.rsqrt(squares), 0.0)

    def rows_of(line):
        return jnp.concatenate([line[:, m * maps : (m + 1) * maps] for m in range(panels)], axis=0)

    side = words_of(rows_of(centre)) + words_of(rows_of(squares)) + words_of(jnp.concatenate(seams, axis=0))[:2]
    side += (jnp.zeros((SIDE - (6 + 4 * RIM) * panels, maps), F32),)
    side = jnp.concatenate(side, axis=0).astype(BF16)
    core = lax.axis_index("core")
    per = maps // (blocks * sum_x)
    for q in range(panels):
        y = (q % halves) * 2 + (core if q < halves else 1 - core)
        by_row = jnp.transpose(jnp.broadcast_to(by_lane[:, q * maps : (q + 1) * maps], (maps, maps)))
        for m in range(halves):
            cols = slice(m * maps, (m + 1) * maps)
            code = encode(gram_ref[pl.ds(q * maps, maps), cols] * by_row * by_lane[:, cols]).astype(BF16)
            for x in range(sum_x):
                for z in range(blocks):
                    at = (z * sum_x + x) * per
                    out_ref[x * sum_y + y, pl.ds((m * blocks + z) * per, per), :] = code[at : at + per]
    for d in range(sum_x * sum_y):
        out_ref[d, pl.ds(halves * blocks * per, SIDE), :] = side


def partial_gram(own, other, mine, square, blocks, halves, pairs, sum_y, sum_x):
    bins = own.shape[1] - 16
    total = 2 * halves * 128
    per = 128 // (blocks * sum_x)
    vmem = pl.BlockSpec(memory_space=pltpu.VMEM)
    return pl.pallas_call(
        lambda *refs: gram_kernel(blocks, halves, pairs, sum_y, sum_x, bins, *refs),
        in_specs=[vmem] * 4,
        out_specs=vmem,
        out_shape=jax.ShapeDtypeStruct((sum_y * sum_x, halves * blocks * per + SIDE, 128), BF16),
        scratch_shapes=[
            pltpu.VMEM((blocks * pairs * bins, total // 2), BF16),
            pltpu.VMEM((blocks * pairs, total), F32),
            pltpu.VMEM((total, total // 2), F32),
        ],
        compiler_params=params(),
        name="partial_gram",
    )(own, other, mine, square)


def sum_kernel(
    blocks, halves, pairs, sum_y, sum_x, count, in_ref, out_ref, mean_ref, scale_ref, between_ref, spread_ref, column_ref
):
    maps = 128
    panels = 2 * halves
    parts = in_ref.shape[0]
    rows = in_ref.shape[1] - SIDE
    per = rows // (halves * blocks)
    tile = per // pairs
    total_bins = float(count * parts)
    squares = jnp.zeros((panels, maps), F32)
    seams = []
    for d in range(parts):
        side = in_ref[d, pl.ds(rows, SIDE), :].astype(F32)
        mean, square = (
            side[i : i + panels] + side[i + panels : i + 2 * panels] + side[i + 2 * panels : i + 3 * panels]
            for i in (0, 3 * panels)
        )
        size = 2 * RIM * panels
        seams.append(side[6 * panels : 6 * panels + size] + side[6 * panels + size : 6 * panels + 2 * size])
        squares = squares + square
        scale = jnp.sqrt(square)
        for m in range(panels):
            mean_ref[d : d + 1, m * maps : (m + 1) * maps] = mean[m : m + 1]
            scale_ref[d : d + 1, m * maps : (m + 1) * maps] = scale[m : m + 1]
    for y in range(sum_y):
        seam = seams[(sum_x - 1) * sum_y + y] + seams[(y + 1) % sum_y]
        for m in range(panels):
            mean_ref[pl.ds(parts + 2 * RIM * y, 2 * RIM), m * maps : (m + 1) * maps] = seam[
                2 * RIM * m : 2 * RIM * (m + 1)
            ]
    means = mean_ref[...]
    row = lax.broadcasted_iota(jnp.int32, (means.shape[0], 1), 0)
    weight = jnp.where(row < parts, float(count), 1.0)
    weight = jnp.where(row < sum_y, float(count - 2 * RIM), weight)
    dev = means - jnp.sum(means * weight, axis=0, keepdims=True) * (1.0 / total_bins)
    own = jnp.concatenate([squares[m : m + 1] for m in range(panels)], axis=1)
    spread = (own + jnp.sum(dev * dev * weight, axis=0, keepdims=True)) * (1.0 / total_bins)
    scales = scale_ref[...]
    y = lax.axis_index("y")
    x = lax.axis_index("xh")
    rows_panel = y // 2 + jnp.where(y % 2 == lax.axis_index("core"), 0, halves)
    for m in range(panels):

        @pl.when(rows_panel == m)
        def _():
            cols = slice(m * maps, (m + 1) * maps)
            between_ref[...] = dot_tn(dev[:, cols] * weight, dev[:, : halves * maps])
            spread_ref[...] = jnp.transpose(jnp.broadcast_to(spread[:, cols], (maps, maps)))
            column = jnp.concatenate([scales[:, cols], jnp.zeros((maps - parts, maps), F32)], axis=0)
            column_ref[...] = jnp.transpose(column)

    for z in range(blocks):
        spot = pl.ds(pl.multiple_of((z * sum_x + x) * per, per), per)
        column = column_ref[spot, :]
        acc = [between_ref[spot, m * maps : (m + 1) * maps] for m in range(halves)]
        for d in range(parts):
            by_row = jnp.broadcast_to(column[:, d : d + 1], (per, maps))
            for m in range(halves):
                code = in_ref[d, pl.ds((m * blocks + z) * per, per), :].astype(F32)
                by_lane = scales[d : d + 1, m * maps : (m + 1) * maps]
                acc[m] = acc[m] + decode(code) * by_row * by_lane
        for m in range(halves):
            bottom = jnp.sqrt(spread_ref[spot, :] * spread[:, m * maps : (m + 1) * maps])
            for j in range(pairs):
                dest = place(m, z, j, blocks, pairs)
                part = slice(j * tile, (j + 1) * tile)
                out_ref[dest, pl.ds(0, tile), :] = acc[m][part] * (1.0 / total_bins)
                out_ref[dest, pl.ds(tile, tile), :] = bottom[part]


def summed(received, blocks, halves, pairs, sum_y, sum_x, count):
    parts = received.shape[0]
    tile = (received.shape[1] - SIDE) // (halves * blocks * pairs)
    total = 2 * halves * 128
    vmem = pl.BlockSpec(memory_space=pltpu.VMEM)
    return pl.pallas_call(
        lambda *refs: sum_kernel(blocks, halves, pairs, sum_y, sum_x, count, *refs),
        in_specs=[vmem],
        out_specs=vmem,
        out_shape=jax.ShapeDtypeStruct((halves * blocks * pairs, 2 * tile, 128), F32),
        scratch_shapes=[
            pltpu.VMEM((parts + 2 * RIM * sum_y, total), F32),
            pltpu.VMEM((parts, total), F32),
            pltpu.VMEM((128, total // 2), F32),
            pltpu.VMEM((128, 128), F32),
            pltpu.VMEM((128, 128), F32),
        ],
        compiler_params=params(),
        name="sum_parts",
    )(received)


def final_kernel(in_ref, gram_ref, scc_ref):
    strata, rows, _ = in_ref.shape
    per = rows // 2
    top = jnp.zeros((per, 128), F32)
    bottom = jnp.zeros((per, 128), F32)
    for k in range(strata):
        tile = in_ref[k, pl.ds(0, per), :]
        gram_ref[:, k, :] = tile
        top = top + tile
        bottom = bottom + in_ref[k, pl.ds(per, per), :]
    scc_ref[...] = top / bottom


def final(received):
    strata, rows, lanes = received.shape
    vmem = pl.BlockSpec(memory_space=pltpu.VMEM)
    return pl.pallas_call(
        final_kernel,
        in_specs=[vmem],
        out_specs=[vmem, vmem],
        out_shape=[
            jax.ShapeDtypeStruct((rows // 2, strata, lanes), F32),
            jax.ShapeDtypeStruct((rows // 2, lanes), F32),
        ],
        compiler_params=params(),
        name="final",
    )(received)


def body(band_maps, stratum_ids, half_width):
    maps, wide, bins = band_maps.shape
    blocks, halves, pairs, sum_y, sum_x = (lax.axis_size(a) for a in ("zl", "zh", "xl", "y", "xh"))
    edge, band_maps = edges(pltpu.with_memory_space_constraint(band_maps, pltpu.HBM))
    behind = lax.ppermute(edge, HALO_AXES, to_next())
    ready = inner(band_maps, stratum_ids, half_width)
    strata = smoothed(*ready, behind, stratum_ids, half_width)
    strata = lax.all_to_all(strata, STRATA_AXES, 0, 0, tiled=True)
    other = lax.ppermute(strata, "core", [(0, 1), (1, 0)])
    own = own_gram(strata, blocks, halves, pairs)
    parts = partial_gram(strata, other, *own, blocks, halves, pairs, sum_y, sum_x)
    parts = lax.all_to_all(parts, SUM_AXES, 0, 0, tiled=True)
    tiles = summed(parts, blocks, halves, pairs, sum_y, sum_x, blocks * pairs * bins)
    tiles = lax.all_to_all(tiles, STRATA_AXES, 0, 0, tiled=True)
    gram, scc = final(tiles)
    return gram, scc


def solution(mesh):
    split = Mesh(mesh.devices.reshape(4, 4, 2, 2, 2, 2), BINS_AXES + MAPS_AXES)
    in_specs = (P(MAPS_AXES, None, BINS_AXES), P(), P())
    out_specs = (P(BINS_AXES, None, MAPS_AXES), P(BINS_AXES, MAPS_AXES))
    return jax.shard_map(body, mesh=split, in_specs=in_specs, out_specs=out_specs, check_vma=False)
```

```python
import jax
import jax.numpy as jnp
from jax import lax
from jax.experimental import pallas as pl
from jax.experimental.pallas import tpu as pltpu
from jax.sharding import Mesh, PartitionSpec as P

HMAX = 2
X_AXES = ("xh", "xl")
BINS_AXES = ("y", "zl") + X_AXES
MAPS_AXES = ("zh", "core")
HALO_AXES = BINS_AXES + ("zh",)
STRATA_AXES = ("zh", "xl", "zl")
SUM_AXES = ("xh", "y")
F32 = jnp.float32
BF16 = jnp.bfloat16
HALO = 4
HEAD = 8
RIM = 2
SIDE = 48
SPAN = 200.0
VMEM_LIMIT = 28 * 1024 * 1024


def place(zh, zl, xl, blocks, pairs):
    return (zh * pairs + xl) * blocks + zl


def to_next():
    zl, x, zh = (lax.axis_size(a) for a in ("zl", X_AXES, "zh"))
    pairs = []
    for y in range(lax.axis_size("y")):
        flat = [((y * zl + p // x % zl) * x + p % x) * zh + p // (x * zl) for p in range(zh * zl * x)]
        pairs += [(flat[p], flat[(p + 1) % len(flat)]) for p in range(len(flat))]
    return pairs


def params():
    return pltpu.CompilerParams(vmem_limit_bytes=VMEM_LIMIT)


def edge_kernel(band_ref, edge_ref, copy_ref, sems):
    maps, wide, bins = band_ref.shape
    copies = [
        pltpu.make_async_copy(band_ref.at[:, :, lanes], copy_ref.at[:, :, lanes], sems.at[half])
        for half, lanes in enumerate((pl.ds(bins - 128, 128), pl.ds(0, bins - 128)))
    ]
    for copy in copies:
        copy.start()
    column = lax.broadcasted_iota(jnp.int32, (128, 128), 0)
    part = lax.rem(lax.broadcasted_iota(jnp.int32, (128, 128), 1), HALO)
    pick = (column == 128 - HALO + part).astype(BF16)
    offset = lax.broadcasted_iota(jnp.int32, (wide, 128), 0)
    lane = lax.broadcasted_iota(jnp.int32, (wide, 128), 1)
    own = (lax.div(lane, HALO) == offset)[None]
    copies[0].wait()
    data = copy_ref[:, :, pl.ds(bins - 128, 128)].reshape(maps * wide, 128)
    spread = jnp.dot(data, pick, preferred_element_type=F32).reshape(maps, wide, 128)
    edge_ref[...] = jnp.sum(jnp.where(own, spread, 0.0), axis=1).astype(BF16)
    copies[1].wait()


def edges(band_maps):
    maps, wide, bins = band_maps.shape
    vmem = pl.BlockSpec(memory_space=pltpu.VMEM)
    return pl.pallas_call(
        edge_kernel,
        in_specs=[pl.BlockSpec(memory_space=pltpu.HBM)],
        out_specs=[vmem, vmem],
        out_shape=[
            jax.ShapeDtypeStruct((maps, 128), BF16),
            jax.ShapeDtypeStruct(band_maps.shape, BF16),
        ],
        scratch_shapes=[pltpu.SemaphoreType.DMA((2,))],
        compiler_params=params(),
        cost_estimate=pl.CostEstimate(flops=2 * maps * wide * 128 * 128, bytes_accessed=2**22, transcendentals=0),
        name="edges",
    )(band_maps)


def windows(planes, win_ref, rows):
    wide = len(planes)
    for mid in range(1, wide - 1):
        one = planes[mid - 1] + planes[mid] + planes[mid + 1]
        win_ref[0, mid, rows, :] = one
        if 2 <= mid < wide - 2:
            win_ref[1, mid, rows, :] = one + (planes[mid - 2] + planes[mid + 2])


def box_of(win_ref, wider, centre):
    h = jnp.where(wider, 1, 0)
    reach = jnp.where(wider, 2, 0)
    outer = jnp.where(wider, 1.0, 0.0)
    scale = jnp.where(wider, 1.0 / 25.0, 1.0 / 9.0)

    def box(at, size):
        acc = win_ref[h, centre, pl.ds(at, size), :]
        acc = acc + win_ref[h, centre + 1, pl.ds(at - 1, size), :]
        acc = acc + win_ref[h, centre - 1, pl.ds(at + 1, size), :]
        far = win_ref[h, centre + reach, pl.ds(at - 2, size), :]
        far = far + win_ref[h, centre - reach, pl.ds(at + 2, size), :]
        return (acc + far * outer) * scale

    return box


def inner_kernel(
    ids_ref, half_ref, band_ref, sums_ref, total_ref, first_win_ref, last_win_ref, plane_ref, turned_ref, win_ref, perm_ref
):
    maps, wide, bins = band_ref.shape
    strata = sums_ref.shape[0]
    r = lax.broadcasted_iota(jnp.int32, (8 * wide, 8 * wide), 0)
    c = lax.broadcasted_iota(jnp.int32, (8 * wide, 8 * wide), 1)
    perm_ref[...] = (c == lax.rem(r, 8) * wide + lax.div(r, 8)).astype(BF16)
    for g in range(0, maps, 16):
        pair = [
            jnp.dot(
                perm_ref[...], band_ref[pl.ds(g + 8 * j, 8)].reshape(8 * wide, bins), preferred_element_type=F32
            ).reshape(wide, 8, bins)
            for j in range(2)
        ]
        plane_ref[:, pl.ds(g, 16), :] = jnp.concatenate(pair, axis=1).astype(BF16)

    for d in range(wide):
        for half in range(bins // 128):
            tile = plane_ref[d, :, half * 128 : half * 128 + 128]
            turned_ref[d, pl.ds(half * 128, 128), :] = jnp.transpose(tile).astype(F32)

    def some(i, carry):
        rows = pl.ds(pl.multiple_of(i * 16, 16), 16)
        windows([turned_ref[d, rows, :] for d in range(wide)], win_ref, rows)
        return carry

    lax.fori_loop(0, bins // 16, some, 0)
    first_win_ref[...] = win_ref[:, :, pl.ds(0, 8), :]
    last_win_ref[...] = win_ref[:, :, pl.ds(bins - 8, 8), :]

    def stratum(k, carry):
        box = box_of(win_ref, half_ref[k] >= 2, ids_ref[k])
        total = jnp.zeros((1, maps), F32)
        for at in range(0, bins - HEAD, 64):
            size = min(64, bins - HEAD - at)
            part = box(at + HEAD - RIM, size)
            sums_ref[k, pl.ds(at, size), :] = part
            total = total + jnp.sum(part, axis=0, keepdims=True)
        total_ref[k] = jnp.broadcast_to(total, (8, maps))
        return carry

    lax.fori_loop(0, strata, stratum, 0, unroll=4)


def inner(band_maps, stratum_ids, half_width):
    maps, wide, bins = band_maps.shape
    strata = stratum_ids.shape[0]
    smem = pl.BlockSpec(memory_space=pltpu.SMEM)
    vmem = pl.BlockSpec(memory_space=pltpu.VMEM)
    return pl.pallas_call(
        inner_kernel,
        in_specs=[smem, smem, vmem],
        out_specs=[vmem, vmem, vmem, vmem],
        out_shape=[
            jax.ShapeDtypeStruct((strata, bins - HEAD, maps), F32),
            jax.ShapeDtypeStruct((strata, 8, maps), F32),
            jax.ShapeDtypeStruct((2, wide, 8, maps), F32),
            jax.ShapeDtypeStruct((2, wide, 8, maps), F32),
        ],
        scratch_shapes=[
            pltpu.VMEM((wide, maps, bins), BF16),
            pltpu.VMEM((wide, bins, maps), F32),
            pltpu.VMEM((2, wide, bins, maps), F32),
            pltpu.VMEM((8 * wide, 8 * wide), BF16),
        ],
        compiler_params=params(),
        cost_estimate=pl.CostEstimate(flops=2 * maps * wide * bins * 256, bytes_accessed=2**22, transcendentals=0),
        name="inner",
    )(stratum_ids, half_width, band_maps)


def words_of(value):
    hi = value.astype(BF16).astype(F32)
    mid = (value - hi).astype(BF16).astype(F32)
    return hi, mid, value - hi - mid


def smooth_kernel(
    ids_ref, half_ref, sums_ref, total_ref, first_win_ref, last_win_ref, behind_ref, out_ref, start_ref, stop_ref
):
    strata, ready, maps = sums_ref.shape
    wide = first_win_ref.shape[1]
    bins = ready + HEAD
    y, z, x = (lax.axis_index(a) for a in ("y", "zl", X_AXES))
    last_y, last_z, last_x = (lax.axis_size(a) - 1 for a in ("y", "zl", X_AXES))
    before = (z == last_z) & (x == last_x)
    after = (z == 0) & (x == 0)
    behind = jnp.where(after, 0.0, jnp.transpose(behind_ref[...].astype(F32)))
    row8 = lax.broadcasted_iota(jnp.int32, (8, maps), 0)
    heads = []
    for d in range(wide):
        at = HALO * d
        tile = pltpu.roll(behind[at // 8 * 8 : at // 8 * 8 + 8], (8 - HALO - at % 8) % 8, axis=0)
        heads.append(jnp.where(row8 >= 8 - HALO, tile, 0.0))
    windows(heads, start_ref, pl.ds(0, 8))
    start_ref[:, :, pl.ds(8, 8), :] = first_win_ref[...]
    stop_ref[:, :, pl.ds(0, 8), :] = last_win_ref[...]
    stop_ref[:, :, pl.ds(8, 8), :] = jnp.zeros((2, wide, 8, maps), F32)

    row = lax.broadcasted_iota(jnp.int32, (16, maps), 0)
    empty = after & (row8 < 2 * RIM)
    seam_before = before & (row8 < 2 * RIM) & ((y < last_y) | (row8 < RIM))
    seam_after = after & (row8 < 2 * RIM) & ((y > 0) | (row8 >= RIM))
    per_slot = jnp.where(after, 1.0 / (bins - 2 * RIM), 1.0 / bins)

    def stratum(k, carry):
        wider, centre = half_ref[k] >= 2, ids_ref[k]
        head = box_of(start_ref, wider, centre)(8 - RIM, 8)
        total = total_ref[k][:1] + jnp.sum(jnp.where(empty, 0.0, head), axis=0, keepdims=True)
        mean = total * per_slot
        square = jnp.zeros((1, maps), F32)
        for at in range(0, bins, 64):
            if at == 0:
                part = [jnp.where(empty, mean, head), sums_ref[k, pl.ds(0, 64 - HEAD), :]]
                part = jnp.concatenate(part, axis=0)
            else:
                part = sums_ref[k, pl.ds(at - HEAD, 64), :]
            part = part - mean
            square = square + jnp.sum(part * part, axis=0, keepdims=True)
            out_ref[k, pl.ds(at, 64), :] = part.astype(BF16)
        seam = jnp.where(seam_before, box_of(stop_ref, wider, centre)(8 - RIM, 8), 0.0)
        seam = seam + jnp.where(seam_after, head, 0.0)
        side = jnp.zeros((16, maps), F32)
        for i, value in enumerate(words_of(mean) + words_of(square)):
            side = jnp.where(row == i, value, side)
        for i, value in enumerate(words_of(seam)[:2]):
            value = jnp.concatenate([value, jnp.zeros((8, maps), F32)], axis=0)
            side = side + pltpu.roll(value, 6 + 2 * RIM * i, axis=0)
        out_ref[k, pl.ds(bins, 16), :] = side.astype(BF16)
        return carry

    lax.fori_loop(0, strata, stratum, 0, unroll=4)


def smoothed(sums, total, first_win, last_win, behind, stratum_ids, half_width):
    strata, ready, maps = sums.shape
    wide = first_win.shape[1]
    smem = pl.BlockSpec(memory_space=pltpu.SMEM)
    vmem = pl.BlockSpec(memory_space=pltpu.VMEM)
    return pl.pallas_call(
        smooth_kernel,
        in_specs=[smem, smem] + [vmem] * 5,
        out_specs=vmem,
        out_shape=jax.ShapeDtypeStruct((strata, ready + HEAD + 16, maps), BF16),
        scratch_shapes=[
            pltpu.VMEM((2, wide, 16, maps), F32),
            pltpu.VMEM((2, wide, 16, maps), F32),
        ],
        compiler_params=params(),
        name="smooth",
    )(stratum_ids, half_width, sums, total, first_win, last_win, behind)


def encode(r):
    size = jnp.exp2(jnp.abs(r) * SPAN - 0.5 * SPAN)
    return jnp.where(r < 0.0, -size, size)


def decode(code):
    size = jnp.log2(jnp.abs(code)) * (1.0 / SPAN) + 0.5
    return jnp.where(code < 0.0, -size, size)


def share(left, rows):
    bin = lax.rem(lax.broadcasted_iota(jnp.int32, (rows, 128), 0), 2 * RIM).astype(F32)
    part = 0.9 - bin * (0.8 / (2 * RIM - 1))
    return jnp.where(left, part, 1.0 - part)


def dot_tn(a, b):
    return lax.dot_general(
        a, b, (((0,), (0,)), ((), ())), precision=lax.Precision.HIGHEST, preferred_element_type=F32
    )


TN = (((0,), (0,)), ((), ()))


def gather_panels(in_ref, data_ref, blocks, halves, pairs, bins):
    for m in range(halves):
        for z in range(blocks):
            for x in range(pairs):
                src = place(m, z, x, blocks, pairs)
                rows = pl.ds((z * pairs + x) * bins, bins)
                data_ref[rows, pl.ds(m * 128, 128)] = in_ref[src, pl.ds(0, bins), :]


def own_kernel(blocks, halves, pairs, bins, own_ref, data_ref, gram_ref):
    gather_panels(own_ref, data_ref, blocks, halves, pairs, bins)
    data = data_ref[...]
    gram_ref[...] = lax.dot_general(data, data, TN, preferred_element_type=F32)


def own_gram(own, blocks, halves, pairs):
    bins = own.shape[1] - 16
    rows, mine = blocks * pairs * bins, halves * 128
    vmem = pl.BlockSpec(memory_space=pltpu.VMEM)
    return pl.pallas_call(
        lambda *refs: own_kernel(blocks, halves, pairs, bins, *refs),
        in_specs=[vmem],
        out_specs=[vmem, vmem],
        out_shape=[jax.ShapeDtypeStruct((rows, mine), BF16), jax.ShapeDtypeStruct((mine, mine), F32)],
        compiler_params=params(),
        cost_estimate=pl.CostEstimate(flops=2 * rows * mine * mine, bytes_accessed=2**21, transcendentals=0),
        name="own_gram",
    )(own)


def gram_kernel(
    blocks, halves, pairs, sum_y, sum_x, bins, own_ref, other_ref, mine_ref, square_ref, out_ref, data_ref, mean_ref, gram_ref
):
    maps = 128
    panels = 2 * halves
    total = panels * maps
    mine = halves * maps
    count_blocks = blocks * pairs
    gather_panels(other_ref, data_ref, blocks, halves, pairs, bins)
    squares, seams = [], []
    for m in range(panels):
        in_ref = (own_ref, other_ref)[m // halves]
        square, seam = [], []
        for z in range(blocks):
            for x in range(pairs):
                src = place(m % halves, z, x, blocks, pairs)
                b = z * pairs + x
                words = in_ref[src, pl.ds(bins, 16), :].astype(F32)
                mean_ref[b : b + 1, m * maps : (m + 1) * maps] = words[0:1] + words[1:2] + words[2:3]
                square.append(words[3:4] + words[4:5] + words[5:6])
                seam.append(words[6:10] + words[10:14])
        squares.append(sum(square))
        seams.append(sum(seam))
    means = mean_ref[...]
    short = lax.axis_index("xh") == 0
    b = lax.broadcasted_iota(jnp.int32, (count_blocks, 1), 0)
    count = jnp.where(short & (b == 0), float(bins - 2 * RIM), float(bins))
    centre = jnp.sum(means * count, axis=0, keepdims=True)
    centre = centre * jnp.where(short, 1.0 / (count_blocks * bins - 2 * RIM), 1.0 / (count_blocks * bins))
    dev = means - centre
    hi, mid, low = words_of(dev[:, :mine])
    left_hi, left_mid, left_low = words_of(dev * count)
    pad = -6 * count_blocks % 32
    left = [left_hi, left_hi, left_mid, left_mid, left_hi, left_low, jnp.zeros((pad, total), F32)]
    right = [hi, mid, hi, mid, low, hi, jnp.zeros((pad, mine), F32)]
    left, right = (jnp.concatenate(a, axis=0).astype(BF16) for a in (left, right))
    between = lax.dot_general(left, right, TN, preferred_element_type=F32)
    gram_ref[:mine] = square_ref[...] + between[:mine]
    gram_ref[mine:] = between[mine:] + lax.dot_general(
        data_ref[...], mine_ref[...], TN, preferred_element_type=F32
    )
    squares = jnp.concatenate(squares, axis=1) + jnp.sum(dev * dev * count, axis=0, keepdims=True)
    by_lane = jnp.where(squares > 0.0, lax.rsqrt(squares), 0.0)

    def rows_of(line):
        return jnp.concatenate([line[:, m * maps : (m + 1) * maps] for m in range(panels)], axis=0)

    of_mean = jnp.concatenate(
        [jnp.broadcast_to(centre[:, m * maps : (m + 1) * maps], (2 * RIM, maps)) for m in range(panels)], axis=0
    )
    seam = jnp.concatenate(seams, axis=0) - share(lax.axis_index("xh") == sum_x - 1, 2 * RIM * panels) * of_mean
    side = words_of(rows_of(centre)) + words_of(rows_of(squares)) + (seam,)
    side += (jnp.zeros((SIDE - (6 + 2 * RIM) * panels, maps), F32),)
    side = jnp.concatenate(side, axis=0).astype(BF16)
    core = lax.axis_index("core")
    per = maps // (blocks * sum_x)
    for q in range(panels):
        y = (q % halves) * 2 + (core if q < halves else 1 - core)
        by_row = jnp.transpose(jnp.broadcast_to(by_lane[:, q * maps : (q + 1) * maps], (maps, maps)))
        for m in range(halves):
            cols = slice(m * maps, (m + 1) * maps)
            code = encode(gram_ref[pl.ds(q * maps, maps), cols] * by_row * by_lane[:, cols]).astype(BF16)
            for x in range(sum_x):
                for z in range(blocks):
                    at = (z * sum_x + x) * per
                    out_ref[x * sum_y + y, pl.ds((m * blocks + z) * per, per), :] = code[at : at + per]
    for d in range(sum_x * sum_y):
        out_ref[d, pl.ds(halves * blocks * per, SIDE), :] = side


def partial_gram(own, other, mine, square, blocks, halves, pairs, sum_y, sum_x):
    bins = own.shape[1] - 16
    total = 2 * halves * 128
    per = 128 // (blocks * sum_x)
    vmem = pl.BlockSpec(memory_space=pltpu.VMEM)
    return pl.pallas_call(
        lambda *refs: gram_kernel(blocks, halves, pairs, sum_y, sum_x, bins, *refs),
        in_specs=[vmem] * 4,
        out_specs=vmem,
        out_shape=jax.ShapeDtypeStruct((sum_y * sum_x, halves * blocks * per + SIDE, 128), BF16),
        scratch_shapes=[
            pltpu.VMEM((blocks * pairs * bins, total // 2), BF16),
            pltpu.VMEM((blocks * pairs, total), F32),
            pltpu.VMEM((total, total // 2), F32),
        ],
        compiler_params=params(),
        name="partial_gram",
    )(own, other, mine, square)


def sum_kernel(
    blocks, halves, pairs, sum_y, sum_x, count, in_ref, out_ref, mean_ref, scale_ref, between_ref, spread_ref, column_ref
):
    maps = 128
    panels = 2 * halves
    parts = in_ref.shape[0]
    rows = in_ref.shape[1] - SIDE
    per = rows // (halves * blocks)
    tile = per // pairs
    total_bins = float(count * parts)
    squares = jnp.zeros((panels, maps), F32)
    seams = []
    for d in range(parts):
        side = in_ref[d, pl.ds(rows, SIDE), :].astype(F32)
        mean, square = (
            side[i : i + panels] + side[i + panels : i + 2 * panels] + side[i + 2 * panels : i + 3 * panels]
            for i in (0, 3 * panels)
        )
        size = 2 * RIM * panels
        of_mean = jnp.concatenate(
            [jnp.broadcast_to(mean[m : m + 1], (2 * RIM, maps)) for m in range(panels)], axis=0
        )
        seams.append(side[6 * panels : 6 * panels + size] + share(d >= parts - sum_y, size) * of_mean)
        squares = squares + square
        scale = jnp.sqrt(square)
        for m in range(panels):
            mean_ref[d : d + 1, m * maps : (m + 1) * maps] = mean[m : m + 1]
            scale_ref[d : d + 1, m * maps : (m + 1) * maps] = scale[m : m + 1]
    for y in range(sum_y):
        seam = seams[(sum_x - 1) * sum_y + y] + seams[(y + 1) % sum_y]
        for m in range(panels):
            mean_ref[pl.ds(parts + 2 * RIM * y, 2 * RIM), m * maps : (m + 1) * maps] = seam[
                2 * RIM * m : 2 * RIM * (m + 1)
            ]
    means = mean_ref[...]
    row = lax.broadcasted_iota(jnp.int32, (means.shape[0], 1), 0)
    weight = jnp.where(row < parts, float(count), 1.0)
    weight = jnp.where(row < sum_y, float(count - 2 * RIM), weight)
    dev = means - jnp.sum(means * weight, axis=0, keepdims=True) * (1.0 / total_bins)
    own = jnp.concatenate([squares[m : m + 1] for m in range(panels)], axis=1)
    spread = (own + jnp.sum(dev * dev * weight, axis=0, keepdims=True)) * (1.0 / total_bins)
    scales = scale_ref[...]
    y = lax.axis_index("y")
    x = lax.axis_index("xh")
    rows_panel = y // 2 + jnp.where(y % 2 == lax.axis_index("core"), 0, halves)
    for m in range(panels):

        @pl.when(rows_panel == m)
        def _():
            cols = slice(m * maps, (m + 1) * maps)
            between_ref[...] = dot_tn(dev[:, cols] * weight, dev[:, : halves * maps])
            spread_ref[...] = jnp.transpose(jnp.broadcast_to(spread[:, cols], (maps, maps)))
            column = jnp.concatenate([scales[:, cols], jnp.zeros((maps - parts, maps), F32)], axis=0)
            column_ref[...] = jnp.transpose(column)

    for z in range(blocks):
        spot = pl.ds(pl.multiple_of((z * sum_x + x) * per, per), per)
        column = column_ref[spot, :]
        acc = [between_ref[spot, m * maps : (m + 1) * maps] for m in range(halves)]
        for d in range(parts):
            by_row = jnp.broadcast_to(column[:, d : d + 1], (per, maps))
            for m in range(halves):
                code = in_ref[d, pl.ds((m * blocks + z) * per, per), :].astype(F32)
                by_lane = scales[d : d + 1, m * maps : (m + 1) * maps]
                acc[m] = acc[m] + decode(code) * by_row * by_lane
        for m in range(halves):
            bottom = jnp.sqrt(spread_ref[spot, :] * spread[:, m * maps : (m + 1) * maps])
            for j in range(pairs):
                dest = place(m, z, j, blocks, pairs)
                part = slice(j * tile, (j + 1) * tile)
                out_ref[dest, pl.ds(0, tile), :] = acc[m][part] * (1.0 / total_bins)
                out_ref[dest, pl.ds(tile, tile), :] = bottom[part]


def summed(received, blocks, halves, pairs, sum_y, sum_x, count):
    parts = received.shape[0]
    tile = (received.shape[1] - SIDE) // (halves * blocks * pairs)
    total = 2 * halves * 128
    vmem = pl.BlockSpec(memory_space=pltpu.VMEM)
    return pl.pallas_call(
        lambda *refs: sum_kernel(blocks, halves, pairs, sum_y, sum_x, count, *refs),
        in_specs=[vmem],
        out_specs=vmem,
        out_shape=jax.ShapeDtypeStruct((halves * blocks * pairs, 2 * tile, 128), F32),
        scratch_shapes=[
            pltpu.VMEM((parts + 2 * RIM * sum_y, total), F32),
            pltpu.VMEM((parts, total), F32),
            pltpu.VMEM((128, total // 2), F32),
            pltpu.VMEM((128, 128), F32),
            pltpu.VMEM((128, 128), F32),
        ],
        compiler_params=params(),
        name="sum_parts",
    )(received)


def final_kernel(in_ref, gram_ref, scc_ref):
    strata, rows, _ = in_ref.shape
    per = rows // 2
    top = jnp.zeros((per, 128), F32)
    bottom = jnp.zeros((per, 128), F32)
    for k in range(strata):
        tile = in_ref[k, pl.ds(0, per), :]
        gram_ref[:, k, :] = tile
        top = top + tile
        bottom = bottom + in_ref[k, pl.ds(per, per), :]
    scc_ref[...] = top / bottom


def final(received):
    strata, rows, lanes = received.shape
    vmem = pl.BlockSpec(memory_space=pltpu.VMEM)
    return pl.pallas_call(
        final_kernel,
        in_specs=[vmem],
        out_specs=[vmem, vmem],
        out_shape=[
            jax.ShapeDtypeStruct((rows // 2, strata, lanes), F32),
            jax.ShapeDtypeStruct((rows // 2, lanes), F32),
        ],
        compiler_params=params(),
        name="final",
    )(received)


def body(band_maps, stratum_ids, half_width):
    maps, wide, bins = band_maps.shape
    blocks, halves, pairs, sum_y, sum_x = (lax.axis_size(a) for a in ("zl", "zh", "xl", "y", "xh"))
    edge, band_maps = edges(pltpu.with_memory_space_constraint(band_maps, pltpu.HBM))
    behind = lax.ppermute(edge, HALO_AXES, to_next())
    ready = inner(band_maps, stratum_ids, half_width)
    strata = smoothed(*ready, behind, stratum_ids, half_width)
    strata = lax.all_to_all(strata, STRATA_AXES, 0, 0, tiled=True)
    other = lax.ppermute(strata, "core", [(0, 1), (1, 0)])
    own = own_gram(strata, blocks, halves, pairs)
    parts = partial_gram(strata, other, *own, blocks, halves, pairs, sum_y, sum_x)
    parts = lax.all_to_all(parts, SUM_AXES, 0, 0, tiled=True)
    tiles = summed(parts, blocks, halves, pairs, sum_y, sum_x, blocks * pairs * bins)
    tiles = lax.all_to_all(tiles, STRATA_AXES, 0, 0, tiled=True)
    gram, scc = final(tiles)
    return gram, scc


def solution(mesh):
    split = Mesh(mesh.devices.reshape(4, 4, 2, 2, 2, 2), BINS_AXES + MAPS_AXES)
    in_specs = (P(MAPS_AXES, None, BINS_AXES), P(), P())
    out_specs = (P(BINS_AXES, None, MAPS_AXES), P(BINS_AXES, MAPS_AXES))
    return jax.shard_map(body, mesh=split, in_specs=in_specs, out_specs=out_specs, check_vma=False)
```

```python
import jax
import jax.numpy as jnp
from jax import lax
from jax.experimental import pallas as pl
from jax.experimental.pallas import tpu as pltpu
from jax.sharding import Mesh, PartitionSpec as P

HMAX = 2
X_AXES = ("xh", "xl")
BINS_AXES = ("y", "zl") + X_AXES
MAPS_AXES = ("zh", "core")
HALO_AXES = BINS_AXES + ("zh",)
STRATA_AXES = ("zh", "xl", "zl")
SUM_AXES = ("xh", "y")
F32 = jnp.float32
BF16 = jnp.bfloat16
HALO = 4
HEAD = 8
RIM = 2
SIDE = 48
SPAN = 200.0
VMEM_LIMIT = 28 * 1024 * 1024


def place(zh, zl, xl, blocks, pairs):
    return (zh * pairs + xl) * blocks + zl


def to_next():
    zl, x, zh = (lax.axis_size(a) for a in ("zl", X_AXES, "zh"))
    pairs = []
    for y in range(lax.axis_size("y")):
        flat = [((y * zl + p // x % zl) * x + p % x) * zh + p // (x * zl) for p in range(zh * zl * x)]
        pairs += [(flat[p], flat[(p + 1) % len(flat)]) for p in range(len(flat))]
    return pairs


def params():
    return pltpu.CompilerParams(vmem_limit_bytes=VMEM_LIMIT)


def edge_kernel(band_ref, edge_ref, copy_ref, sems):
    maps, wide, bins = band_ref.shape
    copies = [
        pltpu.make_async_copy(band_ref.at[:, :, lanes], copy_ref.at[:, :, lanes], sems.at[half])
        for half, lanes in enumerate((pl.ds(bins - 128, 128), pl.ds(0, bins - 128)))
    ]
    for copy in copies:
        copy.start()
    column = lax.broadcasted_iota(jnp.int32, (128, 128), 0)
    part = lax.rem(lax.broadcasted_iota(jnp.int32, (128, 128), 1), HALO)
    pick = (column == 128 - HALO + part).astype(BF16)
    offset = lax.broadcasted_iota(jnp.int32, (wide, 128), 0)
    lane = lax.broadcasted_iota(jnp.int32, (wide, 128), 1)
    own = (lax.div(lane, HALO) == offset)[None]
    copies[0].wait()
    data = copy_ref[:, :, pl.ds(bins - 128, 128)].reshape(maps * wide, 128)
    spread = jnp.dot(data, pick, preferred_element_type=F32).reshape(maps, wide, 128)
    edge_ref[...] = jnp.sum(jnp.where(own, spread, 0.0), axis=1).astype(BF16)
    copies[1].wait()


def edges(band_maps):
    maps, wide, bins = band_maps.shape
    vmem = pl.BlockSpec(memory_space=pltpu.VMEM)
    return pl.pallas_call(
        edge_kernel,
        in_specs=[pl.BlockSpec(memory_space=pltpu.HBM)],
        out_specs=[vmem, vmem],
        out_shape=[
            jax.ShapeDtypeStruct((maps, 128), BF16),
            jax.ShapeDtypeStruct(band_maps.shape, BF16),
        ],
        scratch_shapes=[pltpu.SemaphoreType.DMA((2,))],
        compiler_params=params(),
        cost_estimate=pl.CostEstimate(flops=2 * maps * wide * 128 * 128, bytes_accessed=2**22, transcendentals=0),
        name="edges",
    )(band_maps)


def windows(planes, win_ref, rows):
    wide = len(planes)
    for mid in range(1, wide - 1):
        one = planes[mid - 1] + planes[mid] + planes[mid + 1]
        win_ref[0, mid, rows, :] = one
        if 2 <= mid < wide - 2:
            win_ref[1, mid, rows, :] = one + (planes[mid - 2] + planes[mid + 2])


def box_of(win_ref, wider, centre):
    h = jnp.where(wider, 1, 0)
    reach = jnp.where(wider, 2, 0)
    outer = jnp.where(wider, 1.0, 0.0)
    scale = jnp.where(wider, 1.0 / 25.0, 1.0 / 9.0)

    def box(at, size):
        acc = win_ref[h, centre, pl.ds(at, size), :]
        acc = acc + win_ref[h, centre + 1, pl.ds(at - 1, size), :]
        acc = acc + win_ref[h, centre - 1, pl.ds(at + 1, size), :]
        far = win_ref[h, centre + reach, pl.ds(at - 2, size), :]
        far = far + win_ref[h, centre - reach, pl.ds(at + 2, size), :]
        return (acc + far * outer) * scale

    return box


def inner_kernel(
    ids_ref, half_ref, band_ref, sums_ref, total_ref, first_win_ref, last_win_ref, plane_ref, turned_ref, win_ref, perm_ref
):
    maps, wide, bins = band_ref.shape
    strata = sums_ref.shape[0]
    r = lax.broadcasted_iota(jnp.int32, (8 * wide, 8 * wide), 0)
    c = lax.broadcasted_iota(jnp.int32, (8 * wide, 8 * wide), 1)
    perm_ref[...] = (c == lax.rem(r, 8) * wide + lax.div(r, 8)).astype(BF16)
    for g in range(0, maps, 16):
        pair = [
            jnp.dot(
                perm_ref[...], band_ref[pl.ds(g + 8 * j, 8)].reshape(8 * wide, bins), preferred_element_type=F32
            ).reshape(wide, 8, bins)
            for j in range(2)
        ]
        plane_ref[:, pl.ds(g, 16), :] = jnp.concatenate(pair, axis=1).astype(BF16)

    for d in range(wide):
        for half in range(bins // 128):
            tile = plane_ref[d, :, half * 128 : half * 128 + 128]
            turned_ref[d, pl.ds(half * 128, 128), :] = jnp.transpose(tile).astype(F32)

    def some(i, carry):
        rows = pl.ds(pl.multiple_of(i * 16, 16), 16)
        windows([turned_ref[d, rows, :] for d in range(wide)], win_ref, rows)
        return carry

    lax.fori_loop(0, bins // 16, some, 0, unroll=2)
    first_win_ref[...] = win_ref[:, :, pl.ds(0, 8), :]
    last_win_ref[...] = win_ref[:, :, pl.ds(bins - 8, 8), :]

    def stratum(k, carry):
        box = box_of(win_ref, half_ref[k] >= 2, ids_ref[k])
        total = jnp.zeros((1, maps), F32)
        for at in range(0, bins - HEAD, 128):
            size = min(128, bins - HEAD - at)
            part = box(at + HEAD - RIM, size)
            sums_ref[k, pl.ds(at, size), :] = part
            total = total + jnp.sum(part, axis=0, keepdims=True)
        total_ref[k] = jnp.broadcast_to(total, (8, maps))
        return carry

    lax.fori_loop(0, strata, stratum, 0, unroll=4)


def inner(band_maps, stratum_ids, half_width):
    maps, wide, bins = band_maps.shape
    strata = stratum_ids.shape[0]
    smem = pl.BlockSpec(memory_space=pltpu.SMEM)
    vmem = pl.BlockSpec(memory_space=pltpu.VMEM)
    return pl.pallas_call(
        inner_kernel,
        in_specs=[smem, smem, vmem],
        out_specs=[vmem, vmem, vmem, vmem],
        out_shape=[
            jax.ShapeDtypeStruct((strata, bins - HEAD, maps), F32),
            jax.ShapeDtypeStruct((strata, 8, maps), F32),
            jax.ShapeDtypeStruct((2, wide, 8, maps), F32),
            jax.ShapeDtypeStruct((2, wide, 8, maps), F32),
        ],
        scratch_shapes=[
            pltpu.VMEM((wide, maps, bins), BF16),
            pltpu.VMEM((wide, bins, maps), F32),
            pltpu.VMEM((2, wide, bins, maps), F32),
            pltpu.VMEM((8 * wide, 8 * wide), BF16),
        ],
        compiler_params=params(),
        cost_estimate=pl.CostEstimate(flops=2 * maps * wide * bins * 256, bytes_accessed=2**22, transcendentals=0),
        name="inner",
    )(stratum_ids, half_width, band_maps)


def words_of(value):
    hi = value.astype(BF16).astype(F32)
    mid = (value - hi).astype(BF16).astype(F32)
    return hi, mid, value - hi - mid


def smooth_kernel(
    ids_ref, half_ref, sums_ref, total_ref, first_win_ref, last_win_ref, behind_ref, out_ref, start_ref, stop_ref
):
    strata, ready, maps = sums_ref.shape
    wide = first_win_ref.shape[1]
    bins = ready + HEAD
    y, z, x = (lax.axis_index(a) for a in ("y", "zl", X_AXES))
    last_y, last_z, last_x = (lax.axis_size(a) - 1 for a in ("y", "zl", X_AXES))
    before = (z == last_z) & (x == last_x)
    after = (z == 0) & (x == 0)
    behind = jnp.where(after, 0.0, jnp.transpose(behind_ref[...].astype(F32)))
    row8 = lax.broadcasted_iota(jnp.int32, (8, maps), 0)
    heads = []
    for d in range(wide):
        at = HALO * d
        tile = pltpu.roll(behind[at // 8 * 8 : at // 8 * 8 + 8], (8 - HALO - at % 8) % 8, axis=0)
        heads.append(jnp.where(row8 >= 8 - HALO, tile, 0.0))
    windows(heads, start_ref, pl.ds(0, 8))
    start_ref[:, :, pl.ds(8, 8), :] = first_win_ref[...]
    stop_ref[:, :, pl.ds(0, 8), :] = last_win_ref[...]
    stop_ref[:, :, pl.ds(8, 8), :] = jnp.zeros((2, wide, 8, maps), F32)

    row = lax.broadcasted_iota(jnp.int32, (16, maps), 0)
    empty = after & (row8 < 2 * RIM)
    seam_before = before & (row8 < 2 * RIM) & ((y < last_y) | (row8 < RIM))
    seam_after = after & (row8 < 2 * RIM) & ((y > 0) | (row8 >= RIM))
    per_slot = jnp.where(after, 1.0 / (bins - 2 * RIM), 1.0 / bins)

    def stratum(k, carry):
        wider, centre = half_ref[k] >= 2, ids_ref[k]
        head = box_of(start_ref, wider, centre)(8 - RIM, 8)
        total = total_ref[k][:1] + jnp.sum(jnp.where(empty, 0.0, head), axis=0, keepdims=True)
        mean = total * per_slot
        square = jnp.zeros((1, maps), F32)
        for at in range(0, bins, 64):
            if at == 0:
                part = [jnp.where(empty, mean, head), sums_ref[k, pl.ds(0, 64 - HEAD), :]]
                part = jnp.concatenate(part, axis=0)
            else:
                part = sums_ref[k, pl.ds(at - HEAD, 64), :]
            part = part - mean
            square = square + jnp.sum(part * part, axis=0, keepdims=True)
            out_ref[k, pl.ds(at, 64), :] = part.astype(BF16)
        seam = jnp.where(seam_before, box_of(stop_ref, wider, centre)(8 - RIM, 8), 0.0)
        seam = seam + jnp.where(seam_after, head, 0.0)
        side = jnp.zeros((16, maps), F32)
        for i, value in enumerate(words_of(mean) + words_of(square)):
            side = jnp.where(row == i, value, side)
        for i, value in enumerate(words_of(seam)[:2]):
            value = jnp.concatenate([value, jnp.zeros((8, maps), F32)], axis=0)
            side = side + pltpu.roll(value, 6 + 2 * RIM * i, axis=0)
        out_ref[k, pl.ds(bins, 16), :] = side.astype(BF16)
        return carry

    lax.fori_loop(0, strata, stratum, 0, unroll=4)


def smoothed(sums, total, first_win, last_win, behind, stratum_ids, half_width):
    strata, ready, maps = sums.shape
    wide = first_win.shape[1]
    smem = pl.BlockSpec(memory_space=pltpu.SMEM)
    vmem = pl.BlockSpec(memory_space=pltpu.VMEM)
    return pl.pallas_call(
        smooth_kernel,
        in_specs=[smem, smem] + [vmem] * 5,
        out_specs=vmem,
        out_shape=jax.ShapeDtypeStruct((strata, ready + HEAD + 16, maps), BF16),
        scratch_shapes=[
            pltpu.VMEM((2, wide, 16, maps), F32),
            pltpu.VMEM((2, wide, 16, maps), F32),
        ],
        compiler_params=params(),
        name="smooth",
    )(stratum_ids, half_width, sums, total, first_win, last_win, behind)


def encode(r):
    size = jnp.exp2(jnp.abs(r) * SPAN - 0.5 * SPAN)
    return jnp.where(r < 0.0, -size, size)


def decode(code):
    size = jnp.log2(jnp.abs(code)) * (1.0 / SPAN) + 0.5
    return jnp.where(code < 0.0, -size, size)


def share(left, rows):
    bin = lax.rem(lax.broadcasted_iota(jnp.int32, (rows, 128), 0), 2 * RIM).astype(F32)
    part = 0.9 - bin * (0.8 / (2 * RIM - 1))
    return jnp.where(left, part, 1.0 - part)


def dot_tn(a, b):
    return lax.dot_general(
        a, b, (((0,), (0,)), ((), ())), precision=lax.Precision.HIGHEST, preferred_element_type=F32
    )


TN = (((0,), (0,)), ((), ()))


def gather_panels(in_ref, data_ref, blocks, halves, pairs, bins):
    for m in range(halves):
        for z in range(blocks):
            for x in range(pairs):
                src = place(m, z, x, blocks, pairs)
                rows = pl.ds((z * pairs + x) * bins, bins)
                data_ref[rows, pl.ds(m * 128, 128)] = in_ref[src, pl.ds(0, bins), :]


def own_kernel(blocks, halves, pairs, bins, own_ref, data_ref, gram_ref):
    gather_panels(own_ref, data_ref, blocks, halves, pairs, bins)
    data = data_ref[...]
    gram_ref[...] = lax.dot_general(data, data, TN, preferred_element_type=F32)


def own_gram(own, blocks, halves, pairs):
    bins = own.shape[1] - 16
    rows, mine = blocks * pairs * bins, halves * 128
    vmem = pl.BlockSpec(memory_space=pltpu.VMEM)
    return pl.pallas_call(
        lambda *refs: own_kernel(blocks, halves, pairs, bins, *refs),
        in_specs=[vmem],
        out_specs=[vmem, vmem],
        out_shape=[jax.ShapeDtypeStruct((rows, mine), BF16), jax.ShapeDtypeStruct((mine, mine), F32)],
        compiler_params=params(),
        cost_estimate=pl.CostEstimate(flops=2 * rows * mine * mine, bytes_accessed=2**21, transcendentals=0),
        name="own_gram",
    )(own)


def gram_kernel(
    blocks, halves, pairs, sum_y, sum_x, bins, own_ref, other_ref, mine_ref, square_ref, out_ref, data_ref, mean_ref, gram_ref
):
    maps = 128
    panels = 2 * halves
    total = panels * maps
    mine = halves * maps
    count_blocks = blocks * pairs
    gather_panels(other_ref, data_ref, blocks, halves, pairs, bins)
    squares, seams = [], []
    for m in range(panels):
        in_ref = (own_ref, other_ref)[m // halves]
        square, seam = [], []
        for z in range(blocks):
            for x in range(pairs):
                src = place(m % halves, z, x, blocks, pairs)
                b = z * pairs + x
                words = in_ref[src, pl.ds(bins, 16), :].astype(F32)
                mean_ref[b : b + 1, m * maps : (m + 1) * maps] = words[0:1] + words[1:2] + words[2:3]
                square.append(words[3:4] + words[4:5] + words[5:6])
                seam.append(words[6:10] + words[10:14])
        squares.append(sum(square))
        seams.append(sum(seam))
    means = mean_ref[...]
    short = lax.axis_index("xh") == 0
    b = lax.broadcasted_iota(jnp.int32, (count_blocks, 1), 0)
    count = jnp.where(short & (b == 0), float(bins - 2 * RIM), float(bins))
    centre = jnp.sum(means * count, axis=0, keepdims=True)
    centre = centre * jnp.where(short, 1.0 / (count_blocks * bins - 2 * RIM), 1.0 / (count_blocks * bins))
    dev = means - centre
    hi, mid, low = words_of(dev[:, :mine])
    left_hi, left_mid, left_low = words_of(dev * count)
    pad = -6 * count_blocks % 32
    left = [left_hi, left_hi, left_mid, left_mid, left_hi, left_low, jnp.zeros((pad, total), F32)]
    right = [hi, mid, hi, mid, low, hi, jnp.zeros((pad, mine), F32)]
    left, right = (jnp.concatenate(a, axis=0).astype(BF16) for a in (left, right))
    between = lax.dot_general(left, right, TN, preferred_element_type=F32)
    gram_ref[:mine] = square_ref[...] + between[:mine]
    gram_ref[mine:] = between[mine:] + lax.dot_general(
        data_ref[...], mine_ref[...], TN, preferred_element_type=F32
    )
    squares = jnp.concatenate(squares, axis=1) + jnp.sum(dev * dev * count, axis=0, keepdims=True)
    by_lane = jnp.where(squares > 0.0, lax.rsqrt(squares), 0.0)

    def rows_of(line):
        return jnp.concatenate([line[:, m * maps : (m + 1) * maps] for m in range(panels)], axis=0)

    of_mean = jnp.concatenate(
        [jnp.broadcast_to(centre[:, m * maps : (m + 1) * maps], (2 * RIM, maps)) for m in range(panels)], axis=0
    )
    seam = jnp.concatenate(seams, axis=0) - share(lax.axis_index("xh") == sum_x - 1, 2 * RIM * panels) * of_mean
    side = words_of(rows_of(centre)) + words_of(rows_of(squares)) + (seam,)
    side += (jnp.zeros((SIDE - (6 + 2 * RIM) * panels, maps), F32),)
    side = jnp.concatenate(side, axis=0).astype(BF16)
    core = lax.axis_index("core")
    per = maps // (blocks * sum_x)
    for q in range(panels):
        y = (q % halves) * 2 + (core if q < halves else 1 - core)
        by_row = jnp.transpose(jnp.broadcast_to(by_lane[:, q * maps : (q + 1) * maps], (maps, maps)))
        for m in range(halves):
            cols = slice(m * maps, (m + 1) * maps)
            code = encode(gram_ref[pl.ds(q * maps, maps), cols] * by_row * by_lane[:, cols]).astype(BF16)
            for x in range(sum_x):
                for z in range(blocks):
                    at = (z * sum_x + x) * per
                    out_ref[x * sum_y + y, pl.ds((m * blocks + z) * per, per), :] = code[at : at + per]
    for d in range(sum_x * sum_y):
        out_ref[d, pl.ds(halves * blocks * per, SIDE), :] = side


def partial_gram(own, other, mine, square, blocks, halves, pairs, sum_y, sum_x):
    bins = own.shape[1] - 16
    total = 2 * halves * 128
    per = 128 // (blocks * sum_x)
    vmem = pl.BlockSpec(memory_space=pltpu.VMEM)
    return pl.pallas_call(
        lambda *refs: gram_kernel(blocks, halves, pairs, sum_y, sum_x, bins, *refs),
        in_specs=[vmem] * 4,
        out_specs=vmem,
        out_shape=jax.ShapeDtypeStruct((sum_y * sum_x, halves * blocks * per + SIDE, 128), BF16),
        scratch_shapes=[
            pltpu.VMEM((blocks * pairs * bins, total // 2), BF16),
            pltpu.VMEM((blocks * pairs, total), F32),
            pltpu.VMEM((total, total // 2), F32),
        ],
        compiler_params=params(),
        name="partial_gram",
    )(own, other, mine, square)


def sum_kernel(
    blocks, halves, pairs, sum_y, sum_x, count, in_ref, out_ref, mean_ref, scale_ref, between_ref, spread_ref, column_ref
):
    maps = 128
    panels = 2 * halves
    parts = in_ref.shape[0]
    rows = in_ref.shape[1] - SIDE
    per = rows // (halves * blocks)
    tile = per // pairs
    total_bins = float(count * parts)
    squares = jnp.zeros((panels, maps), F32)
    seams = []
    for d in range(parts):
        side = in_ref[d, pl.ds(rows, SIDE), :].astype(F32)
        mean, square = (
            side[i : i + panels] + side[i + panels : i + 2 * panels] + side[i + 2 * panels : i + 3 * panels]
            for i in (0, 3 * panels)
        )
        size = 2 * RIM * panels
        of_mean = jnp.concatenate(
            [jnp.broadcast_to(mean[m : m + 1], (2 * RIM, maps)) for m in range(panels)], axis=0
        )
        seams.append(side[6 * panels : 6 * panels + size] + share(d >= parts - sum_y, size) * of_mean)
        squares = squares + square
        scale = jnp.sqrt(square)
        for m in range(panels):
            mean_ref[d : d + 1, m * maps : (m + 1) * maps] = mean[m : m + 1]
            scale_ref[d : d + 1, m * maps : (m + 1) * maps] = scale[m : m + 1]
    for y in range(sum_y):
        seam = seams[(sum_x - 1) * sum_y + y] + seams[(y + 1) % sum_y]
        for m in range(panels):
            mean_ref[pl.ds(parts + 2 * RIM * y, 2 * RIM), m * maps : (m + 1) * maps] = seam[
                2 * RIM * m : 2 * RIM * (m + 1)
            ]
    means = mean_ref[...]
    row = lax.broadcasted_iota(jnp.int32, (means.shape[0], 1), 0)
    weight = jnp.where(row < parts, float(count), 1.0)
    weight = jnp.where(row < sum_y, float(count - 2 * RIM), weight)
    dev = means - jnp.sum(means * weight, axis=0, keepdims=True) * (1.0 / total_bins)
    own = jnp.concatenate([squares[m : m + 1] for m in range(panels)], axis=1)
    spread = (own + jnp.sum(dev * dev * weight, axis=0, keepdims=True)) * (1.0 / total_bins)
    scales = scale_ref[...]
    y = lax.axis_index("y")
    x = lax.axis_index("xh")
    rows_panel = y // 2 + jnp.where(y % 2 == lax.axis_index("core"), 0, halves)
    for m in range(panels):

        @pl.when(rows_panel == m)
        def _():
            cols = slice(m * maps, (m + 1) * maps)
            between_ref[...] = dot_tn(dev[:, cols] * weight, dev[:, : halves * maps])
            spread_ref[...] = jnp.transpose(jnp.broadcast_to(spread[:, cols], (maps, maps)))
            column = jnp.concatenate([scales[:, cols], jnp.zeros((maps - parts, maps), F32)], axis=0)
            column_ref[...] = jnp.transpose(column)

    for z in range(blocks):
        spot = pl.ds(pl.multiple_of((z * sum_x + x) * per, per), per)
        column = column_ref[spot, :]
        acc = [between_ref[spot, m * maps : (m + 1) * maps] for m in range(halves)]
        for d in range(parts):
            by_row = jnp.broadcast_to(column[:, d : d + 1], (per, maps))
            for m in range(halves):
                code = in_ref[d, pl.ds((m * blocks + z) * per, per), :].astype(F32)
                by_lane = scales[d : d + 1, m * maps : (m + 1) * maps]
                acc[m] = acc[m] + decode(code) * by_row * by_lane
        for m in range(halves):
            bottom = jnp.sqrt(spread_ref[spot, :] * spread[:, m * maps : (m + 1) * maps])
            for j in range(pairs):
                dest = place(m, z, j, blocks, pairs)
                part = slice(j * tile, (j + 1) * tile)
                out_ref[dest, pl.ds(0, tile), :] = acc[m][part] * (1.0 / total_bins)
                out_ref[dest, pl.ds(tile, tile), :] = bottom[part]


def summed(received, blocks, halves, pairs, sum_y, sum_x, count):
    parts = received.shape[0]
    tile = (received.shape[1] - SIDE) // (halves * blocks * pairs)
    total = 2 * halves * 128
    vmem = pl.BlockSpec(memory_space=pltpu.VMEM)
    return pl.pallas_call(
        lambda *refs: sum_kernel(blocks, halves, pairs, sum_y, sum_x, count, *refs),
        in_specs=[vmem],
        out_specs=vmem,
        out_shape=jax.ShapeDtypeStruct((halves * blocks * pairs, 2 * tile, 128), F32),
        scratch_shapes=[
            pltpu.VMEM((parts + 2 * RIM * sum_y, total), F32),
            pltpu.VMEM((parts, total), F32),
            pltpu.VMEM((128, total // 2), F32),
            pltpu.VMEM((128, 128), F32),
            pltpu.VMEM((128, 128), F32),
        ],
        compiler_params=params(),
        name="sum_parts",
    )(received)


def final_kernel(in_ref, gram_ref, scc_ref):
    strata, rows, _ = in_ref.shape
    per = rows // 2
    top = jnp.zeros((per, 128), F32)
    bottom = jnp.zeros((per, 128), F32)
    for k in range(strata):
        tile = in_ref[k, pl.ds(0, per), :]
        gram_ref[:, k, :] = tile
        top = top + tile
        bottom = bottom + in_ref[k, pl.ds(per, per), :]
    scc_ref[...] = top / bottom


def final(received):
    strata, rows, lanes = received.shape
    vmem = pl.BlockSpec(memory_space=pltpu.VMEM)
    return pl.pallas_call(
        final_kernel,
        in_specs=[vmem],
        out_specs=[vmem, vmem],
        out_shape=[
            jax.ShapeDtypeStruct((rows // 2, strata, lanes), F32),
            jax.ShapeDtypeStruct((rows // 2, lanes), F32),
        ],
        compiler_params=params(),
        name="final",
    )(received)


def body(band_maps, stratum_ids, half_width):
    maps, wide, bins = band_maps.shape
    blocks, halves, pairs, sum_y, sum_x = (lax.axis_size(a) for a in ("zl", "zh", "xl", "y", "xh"))
    edge, band_maps = edges(pltpu.with_memory_space_constraint(band_maps, pltpu.HBM))
    behind = lax.ppermute(edge, HALO_AXES, to_next())
    ready = inner(band_maps, stratum_ids, half_width)
    strata = smoothed(*ready, behind, stratum_ids, half_width)
    strata = lax.all_to_all(strata, STRATA_AXES, 0, 0, tiled=True)
    other = lax.ppermute(strata, "core", [(0, 1), (1, 0)])
    own = own_gram(strata, blocks, halves, pairs)
    parts = partial_gram(strata, other, *own, blocks, halves, pairs, sum_y, sum_x)
    parts = lax.all_to_all(parts, SUM_AXES, 0, 0, tiled=True)
    tiles = summed(parts, blocks, halves, pairs, sum_y, sum_x, blocks * pairs * bins)
    tiles = lax.all_to_all(tiles, STRATA_AXES, 0, 0, tiled=True)
    gram, scc = final(tiles)
    return gram, scc


def solution(mesh):
    split = Mesh(mesh.devices.reshape(4, 4, 2, 2, 2, 2), BINS_AXES + MAPS_AXES)
    in_specs = (P(MAPS_AXES, None, BINS_AXES), P(), P())
    out_specs = (P(BINS_AXES, None, MAPS_AXES), P(BINS_AXES, MAPS_AXES))
    return jax.shard_map(body, mesh=split, in_specs=in_specs, out_specs=out_specs, check_vma=False)
```
